32 devices in a mesh: tok: 16 (over z, y, x), atm: 2 (over core).
Axes of the slice: x: 2, y: 2, z: 4, core: 2. Of those that a mesh axis runs over, the one named last changes fastest.
Arguments:
- pair: bfloat16 [448, 448, 128], P('tok'), may hold values from -6 to 6
- tri_in: bfloat16 [4, 128, 128], replicated, may hold values from -0.5 to 0.5
- tri_gate: bfloat16 [128, 128], replicated, may hold values from -0.5 to 0.5
- tri_out: bfloat16 [128, 128], replicated, may hold values from -0.5 to 0.5
- pair_proj: bfloat16 [128, 16], replicated, may hold values from -0.5 to 0.5
- atom_act: bfloat16 [4096, 128], P(('tok', 'atm')), may hold values from -6 to 6
- atom_cond: bfloat16 [4096, 128], P(('tok', 'atm')), may hold values from -72 to 72
- cond_pair: bfloat16 [2, 128, 16], replicated, may hold values from -0.5 to 0.5
- pair_mlp: bfloat16 [16, 16], replicated, may hold values from -1.5 to 1.5
- bias_proj: bfloat16 [3, 16, 4], replicated, may hold values from -1.5 to 1.5
- block_weights: bfloat16 [3, 7, 128, 128], replicated, may hold values from -0.5 to 0.5
- atom_token: int32 [4096], P(('tok', 'atm')), may hold values from 0 to 447, as said below
- atom_mask: int32 [4096], P(('tok', 'atm')), may hold values from 0 to 1, as said below
- key_start: int32 [128], P(('tok', 'atm')), may hold values from 0 to 3968, as said below
- key_tiles: int32 [128, 40], P(('tok', 'atm')), may hold values from -1 to 447, as said below
Outputs:
- pair_band: bfloat16 [448, 84, 128], P('tok')
- atoms_out: bfloat16 [4096, 128], P(('tok', 'atm'))
The draws below stay inside these ranges and needn't reach their ends.
Inputs may be any that keep to these rules, and one draw needn't show every extreme that they name: `atom_token`: Nondecreasing; atoms 2 * 128 * s to 2 * 128 * s + 2 * 128 - 1 belong to tokens 28 * s to 28 * s + 27, and every token owns 4 atoms or more. `atom_mask`: each token's first atom is valid. key_start[w] is 32 * w - 48 moved by at most 16, clipped to the atoms' range. `key_tiles`: row w lists, rising by one, every token that owns one of window w's key atoms, then -1 in the remaining slots.
All inputs are finite; a program needn't handle non-finite values.
Results may differ from the reference program's by a relative error of at most 0.013.
Values may be sent and summed in bfloat16 or wider, within the bound.
A program may use at most 256 MiB of HBM per device.

```python
import jax
import jax.numpy as jnp
from jax import lax

C = 128
CH = 128
CP = 16
CA = 128
ATTENTION_HEADS = 4
HEAD_CHANNELS = 32
QUERY_ATOMS = 32
KW = 128
KT = 40
AMIN = 4
BLOCKS = 3
TOK_DEV = 28
TOKENS = 448
ATOM_DEV = 128
ATOMS = 4096
WINDOWS = 128


def layout(key):
    shards = TOKENS // TOK_DEV
    span = 2 * ATOM_DEV
    room = span - AMIN * TOK_DEV + TOK_DEV - 1
    shard_keys = jax.random.split(key, shards)

    def one_shard(shard_key):
        picks = jnp.sort(jax.random.permutation(shard_key, room)[:TOK_DEV - 1])
        steps_taken = jnp.arange(TOK_DEV - 1, dtype=jnp.int32)
        starts = picks - steps_taken + AMIN * (steps_taken + 1)
        places = jnp.arange(span, dtype=jnp.int32)
        return jnp.sum((places[:, None] >= starts[None, :]).astype(jnp.int32), 1)
    local = jax.vmap(one_shard)(shard_keys)
    token = (local + (jnp.arange(shards, dtype=jnp.int32) * TOK_DEV)[:, None]).reshape(-1).astype(jnp.int32)
    jitter = jax.random.randint(jax.random.fold_in(key, 11), (WINDOWS,), -16, 17)
    start = jnp.clip(QUERY_ATOMS * jnp.arange(WINDOWS, dtype=jnp.int32) - 48 + jitter, 0, ATOMS - KW).astype(jnp.int32)
    return (token, start)


def draw_atom_token(key, part):
    token, start = layout(key)
    return token


def draw_key_start(key, part):
    token, start = layout(key)
    return start


def draw_key_tiles(key, part):
    token, start = layout(key)
    first = token[start]
    last = token[start + KW - 1]
    listed = first[:, None] + jnp.arange(KT, dtype=jnp.int32)[None, :]
    return jnp.where(listed <= last[:, None], listed, -1).astype(jnp.int32)


def draw_atom_mask(key, part):
    token, start = layout(key)
    key = jax.random.fold_in(key, 5)
    leading = jnp.concatenate([jnp.ones((1,), jnp.bool_), token[1:] != token[:-1]])
    coins = jax.random.randint(key, (ATOMS,), 0, 10) < 8
    return jnp.where(jnp.logical_or(leading, coins), 1, 0).astype(jnp.int32)


def draw_atom_cond(key, part):
    key = jax.random.fold_in(key, 7)
    base = jax.random.normal(key, (ATOMS, CA), jnp.float32)
    values = base
    return jnp.clip(values, -72.0, 72.0).astype(jnp.bfloat16)


def steps_of(rng, extent, cuts, low, top_value):
    level = 1.0
    for dim, shards_of in cuts:
        steps = jax.random.uniform(jax.random.fold_in(jax.random.fold_in(rng, 6), dim), (shards_of,), jnp.float32, low / len(cuts), top_value / len(cuts))
        level = level * jnp.repeat(jnp.exp(steps), extent[dim] // shards_of).reshape((-1,) + (1,) * (len(extent) - 1 - dim))
    return level


def bell_draw(stream_key, dims, width, reach, cuts=(), kind=jnp.bfloat16):
    factor_of = steps_of(stream_key, dims, cuts, -0.22, 0.18) if cuts else 1.0
    drawn = jax.random.normal(stream_key, dims, jnp.float32) * width * factor_of
    return jnp.minimum(jnp.maximum(drawn, -reach), reach).astype(kind)


def setup_inputs(seed: int = 0) -> dict:
    streams_of = jax.random.split(jax.random.key(seed), 16)
    return {
        "pair": bell_draw(streams_of[0], (TOKENS, TOKENS, C), 1.0, 6.0, ((0, 16),)),
        "tri_in": bell_draw(streams_of[1], (4, C, CH), C ** -0.5, 0.5),
        "tri_gate": bell_draw(streams_of[2], (C, C), C ** -0.5, 0.5),
        "tri_out": bell_draw(streams_of[3], (CH, C), CH ** -0.5, 0.5),
        "pair_proj": bell_draw(streams_of[4], (C, CP), C ** -0.5, 0.5),
        "atom_act": bell_draw(streams_of[5], (ATOMS, CA), 1.0, 6.0, ((0, 32),)),
        "atom_cond": draw_atom_cond(jax.random.fold_in(streams_of[15], 71), 0),
        "cond_pair": bell_draw(streams_of[7], (2, CA, CP), CA ** -0.5, 0.5),
        "pair_mlp": bell_draw(streams_of[8], (CP, CP), CP ** -0.5, 1.5),
        "bias_proj": bell_draw(streams_of[9], (BLOCKS, CP, ATTENTION_HEADS), CP ** -0.5, 1.5),
        "block_weights": bell_draw(streams_of[10], (BLOCKS, 7, CA, CA), CA ** -0.5, 0.5),
        "atom_token": draw_atom_token(jax.random.fold_in(streams_of[15], 71), 0),
        "atom_mask": draw_atom_mask(jax.random.fold_in(streams_of[15], 71), 0),
        "key_start": draw_key_start(jax.random.fold_in(streams_of[15], 71), 0),
        "key_tiles": draw_key_tiles(jax.random.fold_in(streams_of[15], 71), 0),
    }


def normalize(values):
    values = values.astype(jnp.float32)
    centred = values - lax.optimization_barrier(jnp.mean(values, -1, keepdims=True))
    return centred * lax.rsqrt(lax.optimization_barrier(jnp.mean(centred * centred, -1, keepdims=True)) + 1e-05)

def project_rows(rows, tri_in):

    def one_row(row):
        normed = normalize(row).astype(jnp.bfloat16)
        parts = [jnp.dot(normed, tri_in[which], preferred_element_type=jnp.float32) for which in range(4)]
        left = (jax.nn.sigmoid(parts[0]) * parts[1]).astype(jnp.bfloat16)
        right = (jax.nn.sigmoid(parts[2]) * parts[3]).astype(jnp.bfloat16)
        return (left, right)
    return lax.map(one_row, rows)

def reference(pair, tri_in, tri_gate, tri_out, pair_proj, atom_act, atom_cond, cond_pair, pair_mlp, bias_proj, block_weights, atom_token, atom_mask, key_start, key_tiles):
    shards = TOKENS // TOK_DEV
    row_groups = pair.reshape(shards, TOK_DEV, TOKENS, C)
    left, right = lax.map(lambda rows: project_rows(rows, tri_in), row_groups)

    def neighbour(which):
        inside = jnp.logical_and(which >= 0, which < shards)
        picked = lax.dynamic_index_in_dim(right, jnp.clip(which, 0, shards - 1), 0, keepdims=False)
        return jnp.where(inside, picked, jnp.zeros_like(picked))

    def shard_band(which):
        beside_all = jnp.concatenate([neighbour(which - 1), neighbour(which), neighbour(which + 1)], 0)
        own_left = lax.dynamic_index_in_dim(left, which, 0, keepdims=False)
        prod = jnp.einsum('ikc,jkc->ijc', own_left.astype(jnp.float32), beside_all.astype(jnp.float32), precision=lax.Precision.HIGHEST)
        rows = lax.dynamic_index_in_dim(row_groups, which, 0, keepdims=False)
        padded = jnp.pad(rows, ((0, 0), (TOK_DEV, TOK_DEV), (0, 0)))
        band = lax.dynamic_slice_in_dim(padded, which * TOK_DEV, 3 * TOK_DEV, 1)
        gate = jax.nn.sigmoid(jnp.dot(normalize(band).astype(jnp.bfloat16), tri_gate, preferred_element_type=jnp.float32))
        update = jnp.dot(normalize(prod).astype(jnp.bfloat16), tri_out, preferred_element_type=jnp.float32)
        band_new = (band.astype(jnp.float32) + gate * update).astype(jnp.bfloat16)
        tok_pair = jnp.dot(normalize(band_new).astype(jnp.bfloat16), pair_proj, preferred_element_type=jnp.float32).astype(jnp.bfloat16)
        return (band_new, tok_pair)
    pair_band, pair_tok = lax.map(shard_band, jnp.arange(shards, dtype=jnp.int32))
    pair_band = pair_band.reshape(TOKENS, 3 * TOK_DEV, C)
    relu_cond = jax.nn.relu(atom_cond)
    query_term = jnp.dot(relu_cond, cond_pair[0], preferred_element_type=jnp.float32)
    key_term = jnp.dot(relu_cond, cond_pair[1], preferred_element_type=jnp.float32)
    mlp_weight = pair_mlp.astype(jnp.float32)

    def window_pair(query_tokens, tiles, start, window_queries):
        home = query_tokens[0] // TOK_DEV
        table = lax.dynamic_index_in_dim(pair_tok, home, 0, keepdims=False)
        rows = query_tokens - home * TOK_DEV
        live = tiles >= 0
        cols = jnp.clip(tiles - (home - 1) * TOK_DEV, 0, 3 * TOK_DEV - 1)
        tiled = table[rows][:, cols]
        tiled = jnp.where(live[None, :, None], tiled, jnp.zeros_like(tiled)).astype(jnp.float32)
        key_tokens = lax.dynamic_slice_in_dim(atom_token, start, KW, 0)
        keys_hot = jnp.logical_and(key_tokens[:, None] == tiles[None, :], live[None, :]).astype(jnp.float32)
        selected = jnp.einsum('lrc,mr->lmc', tiled, keys_hot, precision=lax.Precision.HIGHEST)
        key_rows = lax.dynamic_slice_in_dim(key_term, start, KW, 0)
        pbase = selected + window_queries[:, None, :] + key_rows[None, :, :]
        refined = pbase + jnp.einsum('lmc,cd->lmd', jax.nn.relu(pbase), mlp_weight, precision=lax.Precision.HIGHEST)
        return (refined, lax.dynamic_slice_in_dim(atom_mask, start, KW, 0))
    refined, key_valid = jax.vmap(window_pair)(atom_token.reshape(WINDOWS, QUERY_ATOMS), key_tiles, key_start, query_term.reshape(WINDOWS, QUERY_ATOMS, CP))
    cond_normed = normalize(atom_cond).astype(jnp.bfloat16)
    state = atom_act.astype(jnp.float32)
    for block in range(BLOCKS):
        layer = block_weights[block]
        bias = jnp.einsum('wlmc,ch->whlm', refined, bias_proj[block].astype(jnp.float32), precision=lax.Precision.HIGHEST)
        scale_gate = jax.nn.sigmoid(jnp.dot(cond_normed, layer[0], preferred_element_type=jnp.float32))
        shifted = jnp.dot(cond_normed, layer[1], preferred_element_type=jnp.float32)
        normed = (scale_gate * normalize(state) + shifted).astype(jnp.bfloat16)
        queries = (jnp.dot(normed, layer[2], preferred_element_type=jnp.float32) * HEAD_CHANNELS ** (-0.5)).astype(jnp.bfloat16)
        keys_all = jnp.dot(normed, layer[3], preferred_element_type=jnp.float32).astype(jnp.bfloat16)
        values_all = jnp.dot(normed, layer[4], preferred_element_type=jnp.float32).astype(jnp.bfloat16)
        gates = jax.nn.sigmoid(jnp.dot(normed, layer[5], preferred_element_type=jnp.float32))

        def attend(start, window_queries, pair_bias_rows, valid):
            windowed_key_rows = lax.dynamic_slice_in_dim(keys_all, start, KW, 0).reshape(KW, ATTENTION_HEADS, HEAD_CHANNELS).astype(jnp.float32)
            windowed_value_rows = lax.dynamic_slice_in_dim(values_all, start, KW, 0).reshape(KW, ATTENTION_HEADS, HEAD_CHANNELS).astype(jnp.float32)
            attention_logits = jnp.einsum('fqy,uqy->qfu', window_queries.reshape(QUERY_ATOMS, ATTENTION_HEADS, HEAD_CHANNELS).astype(jnp.float32), windowed_key_rows, precision=lax.Precision.HIGHEST) + pair_bias_rows
            attention_logits = jnp.where(valid[None, None, :] > 0, attention_logits, jnp.float32(-1e+30))
            attention_weights = jax.nn.softmax(attention_logits, -1).astype(jnp.bfloat16)
            blended_output = jnp.einsum('bwv,vbi->wbi', attention_weights.astype(jnp.float32), windowed_value_rows, precision=lax.Precision.HIGHEST)
            return blended_output.reshape(QUERY_ATOMS, CA)
        blended_output = jax.vmap(attend)(key_start, queries.reshape(WINDOWS, QUERY_ATOMS, CA), bias, key_valid).reshape(ATOMS, CA)
        attended = (blended_output * gates).astype(jnp.bfloat16)
        state = state + jnp.dot(attended, layer[6], preferred_element_type=jnp.float32)
    return (pair_band, state.astype(jnp.bfloat16))
```

```python
import functools

import jax
import jax.numpy as jnp
from jax import lax
from jax.experimental import pallas as pl
from jax.experimental.pallas import tpu as pltpu
from jax.sharding import PartitionSpec as P

QUERY_ATOMS = 32
KW = 128
HALO = 64
SLOT = 32
LANES = 128
VMEM_LIMIT = 56 * 1024 * 1024
MESH = pl.DeviceIdType.MESH
NT = (((1,), (1,)), ((), ()))
TN = (((0,), (0,)), ((), ()))


def with_halo(x, sides, width):
    for axis, dim in sides:
        peers, length = (lax.axis_size(axis), x.shape[dim])
        up = [(i, (i + 1) % peers) for i in range(peers - 1)]
        down = [(j, i) for i, j in up]
        last = lax.slice_in_dim(x, length - width, length, axis=dim)
        leading = lax.slice_in_dim(x, 0, width, axis=dim)
        before = lax.ppermute(last, axis, up)
        after = lax.ppermute(leading, axis, down)
        x = jnp.concatenate([before, x, after], axis=dim)
    return x


def sigmoid(x):
    return 0.5 * jnp.tanh(0.5 * x) + 0.5


def normalize(values, axis=-1):
    values = values.astype(jnp.float32)
    centred = values - jnp.mean(values, axis, keepdims=True)
    return centred * lax.rsqrt(jnp.mean(centred * centred, axis, keepdims=True) + 1e-05)


def dot(a, b, dims=None):
    if dims is None:
        return jnp.dot(a, b, preferred_element_type=jnp.float32)
    return lax.dot_general(a, b, dims, preferred_element_type=jnp.float32)


def project_kernel(rows, chunk, lane_tiles, x_ref, w_ref, a_ref, b_ref, a_acc, b_acc):
    step = pl.program_id(1)
    ch = w_ref.shape[0] // 4
    for r in range(rows):
        zn = normalize(x_ref[r]).astype(jnp.bfloat16)
        pad = lane_tiles * LANES - chunk
        if pad:
            zn = jnp.concatenate([zn, jnp.zeros((pad, zn.shape[1]), zn.dtype)], axis=0)
        parts = dot(w_ref[...], zn, NT)
        left = sigmoid(parts[0:ch]) * parts[ch : 2 * ch]
        right = sigmoid(parts[2 * ch : 3 * ch]) * parts[3 * ch : 4 * ch]
        row = step * rows + r
        for q in range(lane_tiles):
            cols = slice(q * LANES, (q + 1) * LANES)
            a_acc[q, pl.ds(row, ch, stride=SLOT), :] = left[:, cols]
            b_acc[q, pl.ds(row, ch, stride=SLOT), :] = right[:, cols]

    @pl.when(step == pl.num_programs(1) - 1)
    def _():
        a_ref[0] = a_acc[...].astype(jnp.bfloat16)
        b_ref[0] = b_acc[...].astype(jnp.bfloat16)


def project(x, w, chunk):
    tok_dev, span, width = x.shape
    ch = w.shape[0] // 4
    rows = 4
    tiles = -(-chunk // LANES)
    shape = (tiles, ch * SLOT, LANES)
    out = jax.ShapeDtypeStruct((span // chunk,) + shape, jnp.bfloat16)
    out_spec = pl.BlockSpec((1,) + shape, lambda k, i: (k, 0, 0, 0))
    return pl.pallas_call(
        functools.partial(project_kernel, rows, chunk, tiles),
        grid=(span // chunk, tok_dev // rows),
        in_specs=[
            pl.BlockSpec((rows, chunk, width), lambda k, i: (i, k, 0)),
            pl.BlockSpec(w.shape, lambda k, i: (0, 0)),
        ],
        out_specs=[out_spec, out_spec],
        out_shape=[out, out],
        scratch_shapes=[pltpu.VMEM(shape, jnp.float32)] * 2,
        compiler_params=pltpu.CompilerParams(vmem_limit_bytes=VMEM_LIMIT),
        cost_estimate=pl.CostEstimate(
            flops=2 * x.size * 4 * ch, bytes_accessed=6 * x.size, transcendentals=2 * x.size
        ),
        name="project",
    )(x, w)


def product_kernel(ch, ao_ref, bo_ref, an_ref, bn_ref, out_ref):
    quarter = ch // 4
    half = ch // 2
    tiles = ao_ref.shape[1]

    @pl.when(pl.program_id(0) == 0)
    def _():
        out_ref[...] = jnp.zeros_like(out_ref)

    def load(ref, at):
        return jnp.concatenate([ref[0, q, pl.ds(at, SLOT), :] for q in range(tiles)], axis=1)

    def group(g, carry):
        outs = []
        for cl in range(4):
            at = pl.multiple_of((cl * quarter + g) * SLOT, SLOT)
            left = jnp.concatenate([load(ao_ref, at), load(an_ref, at)], axis=0)
            right = jnp.concatenate([load(bo_ref, at), load(bn_ref, at)], axis=0)
            outs.append(dot(left, right, NT))
        first = pl.ds(pl.multiple_of(g * SLOT, SLOT), SLOT)
        second = pl.ds(pl.multiple_of((quarter + g) * SLOT, SLOT), SLOT)
        third = pl.ds(pl.multiple_of((half + g) * SLOT, SLOT), SLOT)
        out_ref[first, :] += jnp.concatenate([outs[0][:SLOT], outs[2][:SLOT]], axis=1)
        out_ref[second, :] += jnp.concatenate([outs[1][:SLOT], outs[3][:SLOT]], axis=1)
        out_ref[third, :] += jnp.concatenate([o[SLOT:, :SLOT] for o in outs], axis=1)
        return carry

    lax.fori_loop(0, quarter, group, 0)


def product(own, low, ch):
    chunks, tiles, rows, lanes = own[0].shape
    spec = pl.BlockSpec((1, tiles, rows, lanes), lambda k: (k, 0, 0, 0))
    out_rows = (ch // 2 + ch // 4) * SLOT
    return pl.pallas_call(
        functools.partial(product_kernel, ch),
        grid=(chunks,),
        in_specs=[spec] * 4,
        out_specs=pl.BlockSpec((out_rows, LANES), lambda k: (0, 0)),
        out_shape=jax.ShapeDtypeStruct((out_rows, LANES), jnp.float32),
        compiler_params=pltpu.CompilerParams(vmem_limit_bytes=VMEM_LIMIT),
        name="product",
    )(own[0], own[1], low[0], low[1])


def tail_kernel(rows, tok_dev, ch, p1_ref, p2_ref, d_ref, band_ref, gate_ref, out_w_ref,
                proj_ref, band_out_ref, table_ref):
    step = pl.program_id(0)
    half, quarter = ch // 2, ch // 4
    cp = proj_ref.shape[0]

    @pl.when(step == 0)
    def _():
        table_ref[...] = jnp.zeros_like(table_ref)

    for r in range(rows):
        row = step * rows + r
        near = pl.ds(row, half, stride=SLOT)
        main = p1_ref[near, :] + p2_ref[near, :]
        main = jnp.concatenate([main[:, :64], main[:, 64:]], axis=0)
        above = d_ref[pl.ds(row, quarter, stride=SLOT), :]
        above = jnp.concatenate([above[:, q * SLOT : (q + 1) * SLOT] for q in range(4)], axis=0)
        prod = jnp.concatenate([main, above, above], axis=1)
        pn = normalize(prod, 0).astype(jnp.bfloat16)
        update = dot(pn, out_w_ref[...], TN)
        update = jnp.concatenate(
            [update[SLOT : SLOT + tok_dev], update[:tok_dev], update[64 : 64 + tok_dev]], axis=0
        )
        band = band_ref[r].astype(jnp.float32)
        gate = sigmoid(dot(normalize(band).astype(jnp.bfloat16), gate_ref[...]))
        new = (band + gate * update).astype(jnp.bfloat16)
        band_out_ref[r] = new
        zt = normalize(new)
        zt = jnp.concatenate([zt, jnp.zeros((LANES - 3 * tok_dev, zt.shape[1]), zt.dtype)], axis=0)
        tok = dot(proj_ref[...], zt.astype(jnp.bfloat16), NT)
        table_ref[pl.ds(row, cp, stride=SLOT), :] = tok


def tail(p1, p2, d, band, tri_gate, tri_out, proj_t):
    tok_dev, width, c = band.shape
    ch = tri_out.shape[0]
    cp = proj_t.shape[0]
    rows = 4
    whole = lambda x: pl.BlockSpec(x.shape, lambda i: (0, 0))
    band_spec = pl.BlockSpec((rows, width, c), lambda i: (i, 0, 0))
    return pl.pallas_call(
        functools.partial(tail_kernel, rows, tok_dev, ch),
        grid=(tok_dev // rows,),
        in_specs=[whole(p1), whole(p2), whole(d), band_spec, whole(tri_gate), whole(tri_out),
                  whole(proj_t)],
        out_specs=[band_spec, pl.BlockSpec((cp * SLOT, LANES), lambda i: (0, 0))],
        out_shape=[
            jax.ShapeDtypeStruct(band.shape, jnp.bfloat16),
            jax.ShapeDtypeStruct((cp * SLOT, LANES), jnp.float32),
        ],
        compiler_params=pltpu.CompilerParams(vmem_limit_bytes=VMEM_LIMIT),
        name="tail",
    )(p1, p2, d, band, tri_gate, tri_out, proj_t)


def atom_kernel(devices, heads, blocks, mix_ref, table_ref, qtok_ref, ktok_ref, valid_ref,
                offset_ref, cq_ref, ck_ref, act_ref, cond_ref, w_ref, out_ref,
                ext, bias, planes, send_sem, recv_sem):
    atoms, width = act_ref.shape
    span = atoms + 2 * HALO
    cp = ck_ref.shape[0]
    head_dim = width // heads
    me = lax.axis_index("tok") * 2 + lax.axis_index("atm")
    above, below = me + 1, me - 1
    has_above, has_below = me < devices - 1, me > 0

    def place(d):
        d = jnp.clip(d, 0, devices - 1)
        return (d // 2, d % 2)

    barrier = pltpu.get_barrier_semaphore()

    @pl.when(has_below)
    def _():
        pl.semaphore_signal(barrier, inc=1, device_id=place(below), device_id_type=MESH)

    @pl.when(has_above)
    def _():
        pl.semaphore_signal(barrier, inc=1, device_id=place(above), device_id_type=MESH)

    def copies(b):
        up = pltpu.make_async_remote_copy(
            src_ref=ext.at[b, pl.ds(atoms, HALO)],
            dst_ref=ext.at[b, pl.ds(0, HALO)],
            send_sem=send_sem.at[b, 0],
            recv_sem=recv_sem.at[b, 0],
            device_id=place(above),
            device_id_type=MESH,
        )
        down = pltpu.make_async_remote_copy(
            src_ref=ext.at[b, pl.ds(HALO, HALO)],
            dst_ref=ext.at[b, pl.ds(HALO + atoms, HALO)],
            send_sem=send_sem.at[b, 1],
            recv_sem=recv_sem.at[b, 1],
            device_id=place(below),
            device_id_type=MESH,
        )
        return up, down

    @pl.when(jnp.logical_not(has_below))
    def _():
        for b in range(blocks):
            ext[b, pl.ds(0, HALO)] = jnp.zeros((HALO, width), jnp.bfloat16)

    @pl.when(jnp.logical_not(has_above))
    def _():
        for b in range(blocks):
            ext[b, pl.ds(HALO + atoms, HALO)] = jnp.zeros((HALO, width), jnp.bfloat16)

    cond = normalize(cond_ref[...]).astype(jnp.bfloat16)
    state = act_ref[...].astype(jnp.float32)
    scales = [sigmoid(dot(cond, w_ref[b, 0])) for b in range(blocks)]
    shifts = [dot(cond, w_ref[b, 1]) for b in range(blocks)]

    def begin(b, state):
        normed = (scales[b] * normalize(state) + shifts[b]).astype(jnp.bfloat16)
        ext[b, pl.ds(HALO, atoms)] = normed
        if b == 0:

            @pl.when(jnp.logical_and(has_below, has_above))
            def _():
                pl.semaphore_wait(barrier, 2)

            @pl.when(jnp.logical_not(jnp.logical_and(has_below, has_above)))
            def _():
                pl.semaphore_wait(barrier, 1)

        up, down = copies(b)

        @pl.when(has_above)
        def _():
            up.start()

        @pl.when(has_below)
        def _():
            down.start()

        return normed

    def finish(b):
        up, down = copies(b)

        @pl.when(has_above)
        def _():
            up.wait_send()
            down.wait_recv()

        @pl.when(has_below)
        def _():
            down.wait_send()
            up.wait_recv()

    normed = begin(0, state)

    qhot = (qtok_ref[...] == lax.broadcasted_iota(jnp.int32, (atoms, SLOT), 1)).astype(jnp.float32)
    qhot = qhot.astype(jnp.bfloat16)
    khot = (ktok_ref[...] == lax.broadcasted_iota(jnp.int32, (LANES, span), 0)).astype(jnp.float32)
    khot = khot.astype(jnp.bfloat16)
    picked = dot(table_ref[...].astype(jnp.bfloat16), khot).astype(jnp.bfloat16)
    for c in range(cp):
        sel = dot(qhot, picked[c * SLOT : (c + 1) * SLOT])
        planes[c] = sel + cq_ref[:, c : c + 1] + ck_ref[c : c + 1, :]
    key = lax.broadcasted_iota(jnp.int32, (atoms, span), 1)
    begin_key = offset_ref[...]
    live = jnp.logical_and(key >= begin_key, key < begin_key + KW)
    live = jnp.logical_and(live, valid_ref[...] > 0)
    outs = blocks * heads
    rows = 16

    def mix(g, carry):
        at = pl.ds(pl.multiple_of(g * rows, rows), rows)
        total = [None] * outs
        for c in range(cp):
            base = planes[c, at, :]
            positive = jnp.maximum(base, 0.0)
            for o in range(outs):
                term = base * mix_ref[c, o] + positive * mix_ref[cp + c, o]
                total[o] = term if c == 0 else total[o] + term
        for o in range(outs):
            bias[o, at, :] = total[o]
        return carry

    lax.fori_loop(0, atoms // rows, mix, 0)

    for b in range(blocks):
        if b:
            normed = begin(b, state)
        queries = (dot(normed, w_ref[b, 2]) * head_dim**-0.5).astype(jnp.bfloat16)
        gates = sigmoid(dot(normed, w_ref[b, 5]))
        finish(b)
        full = ext[b]
        keys = dot(full, w_ref[b, 3]).astype(jnp.bfloat16)
        values = dot(full, w_ref[b, 4]).astype(jnp.bfloat16)
        blended = []
        for h in range(heads):
            cols = slice(h * head_dim, (h + 1) * head_dim)
            logits = dot(queries[:, cols], keys[:, cols], NT) + bias[b * heads + h]
            logits = jnp.where(live, logits, -1e30)
            weights = jnp.exp(logits - jnp.max(logits, -1, keepdims=True))
            probs = (weights / jnp.sum(weights, -1, keepdims=True)).astype(jnp.bfloat16)
            blended.append(dot(probs, values[:, cols]))
        attended = (jnp.concatenate(blended, axis=1) * gates).astype(jnp.bfloat16)
        state = state + dot(attended, w_ref[b, 6])
    out_ref[...] = state.astype(jnp.bfloat16)


def atoms_part(mix, table, qtok, ktok, valid, offset, cq, ck, act, cond, weights, devices, heads):
    atoms, width = act.shape
    span = atoms + 2 * HALO
    blocks = weights.shape[0]
    vmem = pl.BlockSpec(memory_space=pltpu.VMEM)
    return pl.pallas_call(
        functools.partial(atom_kernel, devices, heads, blocks),
        in_specs=[pl.BlockSpec(memory_space=pltpu.SMEM)] + [vmem] * 10,
        out_specs=vmem,
        out_shape=jax.ShapeDtypeStruct(act.shape, jnp.bfloat16),
        scratch_shapes=[
            pltpu.VMEM((blocks, span, width), jnp.bfloat16),
            pltpu.VMEM((blocks * heads, atoms, span), jnp.float32),
            pltpu.VMEM((ck.shape[0], atoms, span), jnp.float32),
            pltpu.SemaphoreType.DMA((blocks, 2)),
            pltpu.SemaphoreType.DMA((blocks, 2)),
        ],
        compiler_params=pltpu.CompilerParams(
            collective_id=0, has_side_effects=True, vmem_limit_bytes=VMEM_LIMIT
        ),
        name="atoms",
    )(mix, table, qtok, ktok, valid, offset, cq, ck, act, cond, weights)


def local(
    pair,
    tri_in,
    tri_gate,
    tri_out,
    pair_proj,
    atom_act,
    atom_cond,
    cond_pair,
    pair_mlp,
    bias_proj,
    block_weights,
    atom_token,
    atom_mask,
    key_start,
    key_tiles,
):
    tok_dev, tokens, _ = pair.shape
    groups = lax.axis_size("tok")
    ch = tri_in.shape[2]
    shard = lax.axis_index("tok")
    core = lax.axis_index("atm")
    up = [(i, i + 1) for i in range(groups - 1)]
    down = [(i + 1, i) for i in range(groups - 1)]

    half = tokens // 2
    chunk = 8 * tok_dev
    own = lax.dynamic_slice_in_dim(pair, core * half, half, 1)
    low = lax.ppermute(own, "tok", up)
    w = jnp.swapaxes(tri_in, 1, 2).reshape(4 * ch, -1)
    partial = product(project(own, w, chunk), project(low, w, chunk), ch)
    other = lax.ppermute(partial, "atm", [(0, 1), (1, 0)])
    main_rows = ch // 2 * SLOT
    back = (partial[main_rows:] + other[main_rows:]).astype(jnp.bfloat16)
    back = lax.ppermute(back, "tok", down).astype(jnp.float32)

    padded = jnp.pad(pair, ((0, 0), (tok_dev, tok_dev), (0, 0)))
    band = lax.dynamic_slice_in_dim(padded, shard * tok_dev, 3 * tok_dev, 1)
    pair_band, table = tail(partial, other, back, band, tri_gate, tri_out, pair_proj.T)

    atoms = atom_act.shape[0]
    heads = bias_proj.shape[2]
    device = shard * lax.axis_size("atm") + core
    labels = jnp.stack([atom_token, atom_mask], 1)
    labels_ext = with_halo(labels, ((("tok", "atm"), 0),), HALO)
    relu_cond = jax.nn.relu(atom_cond)
    query_term = jnp.dot(relu_cond, cond_pair[0], preferred_element_type=jnp.float32)
    key_term = jnp.dot(relu_cond, cond_pair[1], preferred_element_type=jnp.float32)
    key_term_ext = with_halo(key_term, ((("tok", "atm"), 0),), HALO)
    offsets = key_start - device * atoms + HALO
    projections = jnp.swapaxes(bias_proj, 0, 1).reshape(bias_proj.shape[1], -1).astype(jnp.float32)
    mixed = jnp.dot(
        pair_mlp.astype(jnp.float32), projections, precision=lax.Precision.HIGHEST
    )
    atoms_out = atoms_part(
        jnp.concatenate([projections, mixed], 0),
        table,
        (atom_token - shard * tok_dev)[:, None],
        (labels_ext[:, 0] - (shard - 1) * tok_dev)[None, :],
        labels_ext[:, 1][None, :],
        jnp.repeat(offsets, QUERY_ATOMS)[:, None],
        query_term,
        key_term_ext.T,
        atom_act,
        atom_cond,
        block_weights,
        groups * lax.axis_size("atm"),
        heads,
    )
    return (pair_band, atoms_out)


def solution(mesh):
    in_specs = (
        P("tok", None, None),
        P(),
        P(),
        P(),
        P(),
        P(("tok", "atm"), None),
        P(("tok", "atm"), None),
        P(),
        P(),
        P(),
        P(),
        P(("tok", "atm")),
        P(("tok", "atm")),
        P(("tok", "atm")),
        P(("tok", "atm"), None),
    )
    out_specs = (P("tok", None, None), P(("tok", "atm"), None))
    return jax.shard_map(local, mesh=mesh, in_specs=in_specs, out_specs=out_specs, check_vma=False)
```

```python
import functools

import jax
import jax.numpy as jnp
from jax import lax
from jax.experimental import pallas as pl
from jax.experimental.pallas import tpu as pltpu
from jax.sharding import PartitionSpec as P

QUERY_ATOMS = 32
KW = 128
HALO = 64
SLOT = 32
PART_SLOT = 16
LANES = 128
VMEM_LIMIT = 56 * 1024 * 1024
MESH = pl.DeviceIdType.MESH
NT = (((1,), (1,)), ((), ()))
TN = (((0,), (0,)), ((), ()))


def with_halo(x, sides, width):
    for axis, dim in sides:
        peers, length = (lax.axis_size(axis), x.shape[dim])
        up = [(i, (i + 1) % peers) for i in range(peers - 1)]
        down = [(j, i) for i, j in up]
        last = lax.slice_in_dim(x, length - width, length, axis=dim)
        leading = lax.slice_in_dim(x, 0, width, axis=dim)
        before = lax.ppermute(last, axis, up)
        after = lax.ppermute(leading, axis, down)
        x = jnp.concatenate([before, x, after], axis=dim)
    return x


def sigmoid(x):
    return 0.5 * jnp.tanh(0.5 * x) + 0.5


def normalize(values, axis=-1):
    values = values.astype(jnp.float32)
    centred = values - jnp.mean(values, axis, keepdims=True)
    return centred * lax.rsqrt(jnp.mean(centred * centred, axis, keepdims=True) + 1e-05)


def dot(a, b, dims=None):
    if dims is None:
        return jnp.dot(a, b, preferred_element_type=jnp.float32)
    return lax.dot_general(a, b, dims, preferred_element_type=jnp.float32)


def project_kernel(rows, chunk, lane_tiles, x_ref, w_ref, a_ref, b_ref, a_acc, b_acc):
    step = pl.program_id(1)
    ch = w_ref.shape[0] // 4
    for r in range(rows):
        zn = normalize(x_ref[r]).astype(jnp.bfloat16)
        pad = lane_tiles * LANES - chunk
        if pad:
            zn = jnp.concatenate([zn, jnp.zeros((pad, zn.shape[1]), zn.dtype)], axis=0)
        parts = dot(w_ref[...], zn, NT)
        left = sigmoid(parts[0:ch]) * parts[ch : 2 * ch]
        right = sigmoid(parts[2 * ch : 3 * ch]) * parts[3 * ch : 4 * ch]
        row = step * rows + r
        for q in range(lane_tiles):
            cols = slice(q * LANES, (q + 1) * LANES)
            a_acc[q, pl.ds(row, ch, stride=PART_SLOT), :] = left[:, cols]
            b_acc[q, pl.ds(row, ch, stride=PART_SLOT), :] = right[:, cols]

    @pl.when(step == pl.num_programs(1) - 1)
    def _():
        a_ref[0] = a_acc[...].astype(jnp.bfloat16)
        b_ref[0] = b_acc[...].astype(jnp.bfloat16)


def project(x, w, chunk):
    part, span, width = x.shape
    ch = w.shape[0] // 4
    rows = part // 2
    tiles = -(-chunk // LANES)
    shape = (tiles, ch * PART_SLOT, LANES)
    out = jax.ShapeDtypeStruct((span // chunk,) + shape, jnp.bfloat16)
    out_spec = pl.BlockSpec((1,) + shape, lambda k, i: (k, 0, 0, 0))
    return pl.pallas_call(
        functools.partial(project_kernel, rows, chunk, tiles),
        grid=(span // chunk, part // rows),
        in_specs=[
            pl.BlockSpec((rows, chunk, width), lambda k, i: (i, k, 0)),
            pl.BlockSpec(w.shape, lambda k, i: (0, 0)),
        ],
        out_specs=[out_spec, out_spec],
        out_shape=[out, out],
        scratch_shapes=[pltpu.VMEM(shape, jnp.float32)] * 2,
        compiler_params=pltpu.CompilerParams(vmem_limit_bytes=VMEM_LIMIT),
        cost_estimate=pl.CostEstimate(
            flops=2 * x.size * 4 * ch, bytes_accessed=16 * x.size, transcendentals=2 * x.size
        ),
        name="project",
    )(x, w)


def product_kernel(ch, a0_ref, a1_ref, b0_ref, b1_ref, out_ref):
    quarter = ch // 4
    tiles = a0_ref.shape[1]

    @pl.when(pl.program_id(0) == 0)
    def _():
        out_ref[...] = jnp.zeros_like(out_ref)

    def load(first, second, at):
        rows = pl.ds(at, PART_SLOT)
        return jnp.concatenate(
            [
                jnp.concatenate([ref[0, q, rows, :] for q in range(tiles)], axis=1)
                for ref in (first, second)
            ],
            axis=0,
        )

    def group(g, carry):
        outs = []
        for cl in range(4):
            at = pl.multiple_of((cl * quarter + g) * PART_SLOT, PART_SLOT)
            outs.append(dot(load(a0_ref, a1_ref, at), load(b0_ref, b1_ref, at), NT))
        out_ref[pl.ds(pl.multiple_of(g * SLOT, SLOT), SLOT), :] += jnp.concatenate(outs, axis=1)
        return carry

    lax.fori_loop(0, quarter, group, 0, unroll=4)


def product(left, right, ch):
    chunks, tiles, rows, lanes = left[0].shape
    spec = pl.BlockSpec((1, tiles, rows, lanes), lambda k: (k, 0, 0, 0))
    out_rows = ch // 4 * SLOT
    return pl.pallas_call(
        functools.partial(product_kernel, ch),
        grid=(chunks,),
        in_specs=[spec] * 4,
        out_specs=pl.BlockSpec((out_rows, LANES), lambda k: (0, 0)),
        out_shape=jax.ShapeDtypeStruct((out_rows, LANES), jnp.float32),
        compiler_params=pltpu.CompilerParams(vmem_limit_bytes=VMEM_LIMIT),
        cost_estimate=pl.CostEstimate(
            flops=2 * SLOT * SLOT * ch * chunks * tiles * lanes,
            bytes_accessed=16 * chunks * tiles * rows * lanes,
            transcendentals=0,
        ),
        name="product",
    )(left[0], left[1], right[0], right[1])


def gate_kernel(band_ref, gate_ref, out_ref):
    rows, width, c = band_ref.shape
    band = band_ref[...].reshape(rows * width, c)
    gate = sigmoid(dot(normalize(band).astype(jnp.bfloat16), gate_ref[...]))
    out_ref[...] = gate.reshape(rows, width, c)


def gates_of(band, tri_gate):
    tok_dev, width, c = band.shape
    rows = 4
    spec = pl.BlockSpec((rows, width, c), lambda i: (i, 0, 0))
    return pl.pallas_call(
        gate_kernel,
        grid=(tok_dev // rows,),
        in_specs=[spec, pl.BlockSpec(tri_gate.shape, lambda i: (0, 0))],
        out_specs=spec,
        out_shape=jax.ShapeDtypeStruct(band.shape, jnp.float32),
        compiler_params=pltpu.CompilerParams(vmem_limit_bytes=VMEM_LIMIT),
        cost_estimate=pl.CostEstimate(
            flops=2 * band.size * c, bytes_accessed=16 * band.size, transcendentals=band.size
        ),
        name="gate",
    )(band, tri_gate)


def tail_kernel(rows, tok_dev, ch, own_ref, m1_ref, m2_ref, d_ref, band_ref, gate_ref, out_w_ref,
                proj_ref, band_out_ref, table_ref):
    step = pl.program_id(0)
    quarter = ch // 4
    part = tok_dev // 2
    cp = proj_ref.shape[0]
    width, c = band_ref.shape[1:]

    @pl.when(step == 0)
    def _():
        table_ref[...] = jnp.zeros_like(table_ref)

    places, updates = [], []
    for r in range(rows):
        row = step * rows + r
        row = row + jnp.where(row >= part, PART_SLOT - part, 0)
        places.append(row)
        near = pl.ds(row, quarter, stride=SLOT)
        packed = [own_ref[near, :], m1_ref[near, :] + m2_ref[near, :], d_ref[near, :]]
        prod = jnp.concatenate(
            [
                jnp.concatenate([p[:, q * SLOT : (q + 1) * SLOT] for p in packed], axis=1)
                for q in range(4)
            ],
            axis=0,
        )
        pn = normalize(prod, 0).astype(jnp.bfloat16)
        updates.append(dot(pn, out_w_ref[...], TN))
    band = band_ref[...].reshape(rows * width, c).astype(jnp.float32)
    gate = gate_ref[...].reshape(rows * width, c)
    new = (band + gate * jnp.concatenate(updates, axis=0)).astype(jnp.bfloat16)
    zt = normalize(new).astype(jnp.bfloat16)
    lane = lax.broadcasted_iota(jnp.int32, (cp, width), 1)
    used = lax.rem(lane, PART_SLOT) < part
    plain = new.astype(jnp.float32)
    for r in range(rows):
        pieces = []
        for slot in (1, 0, 2):
            for half in range(2):
                at = r * width + slot * SLOT + half * PART_SLOT
                pieces.append(plain[at : at + part])
        band_out_ref[r] = jnp.concatenate(pieces, axis=0).astype(jnp.bfloat16)
        tok = dot(proj_ref[...], zt[r * width : (r + 1) * width], NT)
        tok = jnp.where(used, tok, 0.0)
        tok = jnp.concatenate([tok, jnp.zeros((cp, LANES - width), jnp.float32)], axis=1)
        table_ref[pl.ds(places[r], cp, stride=SLOT), :] = tok


def tail(own, m1, m2, d, band, gate, tri_out, proj_t):
    tok_dev, width, c = band.shape
    ch = tri_out.shape[0]
    cp = proj_t.shape[0]
    rows = 4
    whole = lambda x: pl.BlockSpec(x.shape, lambda i: (0, 0))
    band_spec = pl.BlockSpec((rows, width, c), lambda i: (i, 0, 0))
    return pl.pallas_call(
        functools.partial(tail_kernel, rows, tok_dev, ch),
        grid=(tok_dev // rows,),
        in_specs=[whole(own), whole(m1), whole(m2), whole(d), band_spec, band_spec,
                  whole(tri_out), whole(proj_t)],
        out_specs=[
            pl.BlockSpec((rows, 3 * tok_dev, c), lambda i: (i, 0, 0)),
            pl.BlockSpec((cp * SLOT, LANES), lambda i: (0, 0)),
        ],
        out_shape=[
            jax.ShapeDtypeStruct((tok_dev, 3 * tok_dev, c), jnp.bfloat16),
            jax.ShapeDtypeStruct((cp * SLOT, LANES), jnp.float32),
        ],
        compiler_params=pltpu.CompilerParams(vmem_limit_bytes=VMEM_LIMIT),
        name="tail",
    )(own, m1, m2, d, band, gate, tri_out, proj_t)


def atom_kernel(devices, heads, blocks, mix_ref, table_ref, qtok_ref, ktok_ref, valid_ref,
                offset_ref, cq_ref, ck_ref, act_ref, cond_ref, w_ref, out_ref,
                ext, bias, planes, send_sem, recv_sem):
    atoms, width = act_ref.shape
    span = atoms + 2 * HALO
    cp = ck_ref.shape[0]
    head_dim = width // heads
    me = lax.axis_index("tok") * 2 + lax.axis_index("atm")
    above, below = me + 1, me - 1
    has_above, has_below = me < devices - 1, me > 0

    def place(d):
        d = jnp.clip(d, 0, devices - 1)
        return (d // 2, d % 2)

    barrier = pltpu.get_barrier_semaphore()

    @pl.when(has_below)
    def _():
        pl.semaphore_signal(barrier, inc=1, device_id=place(below), device_id_type=MESH)

    @pl.when(has_above)
    def _():
        pl.semaphore_signal(barrier, inc=1, device_id=place(above), device_id_type=MESH)

    def copies(b):
        up = pltpu.make_async_remote_copy(
            src_ref=ext.at[b, pl.ds(atoms, HALO)],
            dst_ref=ext.at[b, pl.ds(0, HALO)],
            send_sem=send_sem.at[b, 0],
            recv_sem=recv_sem.at[b, 0],
            device_id=place(above),
            device_id_type=MESH,
        )
        down = pltpu.make_async_remote_copy(
            src_ref=ext.at[b, pl.ds(HALO, HALO)],
            dst_ref=ext.at[b, pl.ds(HALO + atoms, HALO)],
            send_sem=send_sem.at[b, 1],
            recv_sem=recv_sem.at[b, 1],
            device_id=place(below),
            device_id_type=MESH,
        )
        return up, down

    @pl.when(jnp.logical_not(has_below))
    def _():
        for b in range(blocks):
            ext[b, pl.ds(0, HALO)] = jnp.zeros((HALO, width), jnp.bfloat16)

    @pl.when(jnp.logical_not(has_above))
    def _():
        for b in range(blocks):
            ext[b, pl.ds(HALO + atoms, HALO)] = jnp.zeros((HALO, width), jnp.bfloat16)

    cond = normalize(cond_ref[...]).astype(jnp.bfloat16)
    state = act_ref[...].astype(jnp.float32)
    scales = [sigmoid(dot(cond, w_ref[b, 0])) for b in range(blocks)]
    shifts = [dot(cond, w_ref[b, 1]) for b in range(blocks)]

    def begin(b, state):
        normed = (scales[b] * normalize(state) + shifts[b]).astype(jnp.bfloat16)
        ext[b, pl.ds(HALO, atoms)] = normed
        if b == 0:

            @pl.when(jnp.logical_and(has_below, has_above))
            def _():
                pl.semaphore_wait(barrier, 2)

            @pl.when(jnp.logical_not(jnp.logical_and(has_below, has_above)))
            def _():
                pl.semaphore_wait(barrier, 1)

        up, down = copies(b)

        @pl.when(has_above)
        def _():
            up.start()

        @pl.when(has_below)
        def _():
            down.start()

        return normed

    def finish(b):
        up, down = copies(b)

        @pl.when(has_above)
        def _():
            up.wait_send()
            down.wait_recv()

        @pl.when(has_below)
        def _():
            down.wait_send()
            up.wait_recv()

    normed = begin(0, state)

    qhot = (qtok_ref[...] == lax.broadcasted_iota(jnp.int32, (atoms, SLOT), 1)).astype(jnp.float32)
    qhot = qhot.astype(jnp.bfloat16)
    khot = (ktok_ref[...] == lax.broadcasted_iota(jnp.int32, (LANES, span), 0)).astype(jnp.float32)
    khot = khot.astype(jnp.bfloat16)
    picked = dot(table_ref[...].astype(jnp.bfloat16), khot).astype(jnp.bfloat16)
    for c in range(cp):
        sel = dot(qhot, picked[c * SLOT : (c + 1) * SLOT])
        planes[c] = sel + cq_ref[:, c : c + 1] + ck_ref[c : c + 1, :]
    key = lax.broadcasted_iota(jnp.int32, (atoms, span), 1)
    begin_key = offset_ref[...]
    live = jnp.logical_and(key >= begin_key, key < begin_key + KW)
    live = jnp.logical_and(live, valid_ref[...] > 0)
    outs = blocks * heads
    rows = 16

    def mix(g, carry):
        at = pl.ds(pl.multiple_of(g * rows, rows), rows)
        total = [None] * outs
        for c in range(cp):
            base = planes[c, at, :]
            positive = jnp.maximum(base, 0.0)
            for o in range(outs):
                term = base * mix_ref[c, o] + positive * mix_ref[cp + c, o]
                total[o] = term if c == 0 else total[o] + term
        for o in range(outs):
            bias[o, at, :] = total[o]
        return carry

    lax.fori_loop(0, atoms // rows, mix, 0)

    for b in range(blocks):
        if b:
            normed = begin(b, state)
        queries = (dot(normed, w_ref[b, 2]) * head_dim**-0.5).astype(jnp.bfloat16)
        gates = sigmoid(dot(normed, w_ref[b, 5]))
        finish(b)
        full = ext[b]
        keys = dot(full, w_ref[b, 3]).astype(jnp.bfloat16)
        values = dot(full, w_ref[b, 4]).astype(jnp.bfloat16)
        blended = []
        for h in range(heads):
            cols = slice(h * head_dim, (h + 1) * head_dim)
            logits = dot(queries[:, cols], keys[:, cols], NT) + bias[b * heads + h]
            logits = jnp.where(live, logits, -1e30)
            weights = jnp.exp(logits - jnp.max(logits, -1, keepdims=True))
            probs = (weights / jnp.sum(weights, -1, keepdims=True)).astype(jnp.bfloat16)
            blended.append(dot(probs, values[:, cols]))
        attended = (jnp.concatenate(blended, axis=1) * gates).astype(jnp.bfloat16)
        state = state + dot(attended, w_ref[b, 6])
    out_ref[...] = state.astype(jnp.bfloat16)


def atoms_part(mix, table, qtok, ktok, valid, offset, cq, ck, act, cond, weights, devices, heads):
    atoms, width = act.shape
    span = atoms + 2 * HALO
    blocks = weights.shape[0]
    vmem = pl.BlockSpec(memory_space=pltpu.VMEM)
    return pl.pallas_call(
        functools.partial(atom_kernel, devices, heads, blocks),
        in_specs=[pl.BlockSpec(memory_space=pltpu.SMEM)] + [vmem] * 10,
        out_specs=vmem,
        out_shape=jax.ShapeDtypeStruct(act.shape, jnp.bfloat16),
        scratch_shapes=[
            pltpu.VMEM((blocks, span, width), jnp.bfloat16),
            pltpu.VMEM((blocks * heads, atoms, span), jnp.float32),
            pltpu.VMEM((ck.shape[0], atoms, span), jnp.float32),
            pltpu.SemaphoreType.DMA((blocks, 2)),
            pltpu.SemaphoreType.DMA((blocks, 2)),
        ],
        compiler_params=pltpu.CompilerParams(
            collective_id=0, has_side_effects=True, vmem_limit_bytes=VMEM_LIMIT
        ),
        name="atoms",
    )(mix, table, qtok, ktok, valid, offset, cq, ck, act, cond, weights)


def local(
    pair,
    tri_in,
    tri_gate,
    tri_out,
    pair_proj,
    atom_act,
    atom_cond,
    cond_pair,
    pair_mlp,
    bias_proj,
    block_weights,
    atom_token,
    atom_mask,
    key_start,
    key_tiles,
):
    tok_dev, tokens, _ = pair.shape
    groups = lax.axis_size("tok")
    ch = tri_in.shape[2]
    shard = lax.axis_index("tok")
    core = lax.axis_index("atm")
    up = [(i, i + 1) for i in range(groups - 1)]
    down = [(i + 1, i) for i in range(groups - 1)]

    half = tokens // 2
    part = tok_dev // 2
    chunk = 8 * tok_dev
    own = lax.dynamic_slice_in_dim(pair, core * half, half, 1)
    low0 = lax.ppermute(own[:part], "tok", up)
    low1 = lax.ppermute(own[part:], "tok", up)
    w = jnp.swapaxes(tri_in, 1, 2).reshape(4 * ch, -1)
    own0, own1 = project(own[:part], w, chunk), project(own[part:], w, chunk)
    own_left, own_right = (own0[0], own1[0]), (own0[1], own1[1])
    own_prod = product(own_left, own_right, ch)
    own_prod = own_prod + lax.ppermute(own_prod, "atm", [(0, 1), (1, 0)])

    padded = jnp.pad(pair, ((0, 0), (tok_dev, tok_dev), (0, 0)))
    band = lax.dynamic_slice_in_dim(padded, shard * tok_dev, 3 * tok_dev, 1)
    band = band.reshape(tok_dev, 3, 2, part, -1)
    band = jnp.concatenate([band[:, 1:2], band[:, 0:1], band[:, 2:3]], axis=1)
    band = jnp.pad(band, ((0, 0), (0, 0), (0, 0), (0, PART_SLOT - part), (0, 0)))
    band = band.reshape(tok_dev, 3 * SLOT, -1)
    gate = gates_of(band, tri_gate)

    atoms = atom_act.shape[0]
    heads = bias_proj.shape[2]
    device = shard * lax.axis_size("atm") + core
    labels = jnp.stack([atom_token, atom_mask], 1)
    labels_ext = with_halo(labels, ((("tok", "atm"), 0),), HALO)
    relu_cond = jax.nn.relu(atom_cond)
    query_term = jnp.dot(relu_cond, cond_pair[0], preferred_element_type=jnp.float32)
    key_term = jnp.dot(relu_cond, cond_pair[1], preferred_element_type=jnp.float32)
    key_term_ext = with_halo(key_term, ((("tok", "atm"), 0),), HALO)
    offsets = key_start - device * atoms + HALO
    projections = jnp.swapaxes(bias_proj, 0, 1).reshape(bias_proj.shape[1], -1).astype(jnp.float32)
    mixed = jnp.dot(
        pair_mlp.astype(jnp.float32), projections, precision=lax.Precision.HIGHEST
    )
    spread = PART_SLOT - part
    qtok = atom_token - shard * tok_dev
    qtok = qtok + jnp.where(qtok >= part, spread, 0)
    ktok = labels_ext[:, 0] - (shard - 1) * tok_dev
    kgroup = (ktok >= tok_dev).astype(jnp.int32) + (ktok >= 2 * tok_dev).astype(jnp.int32)
    ktok = ktok - kgroup * tok_dev
    ktok = ktok + jnp.where(ktok >= part, spread, 0)
    ktok = ktok + SLOT * jnp.where(kgroup == 0, 1, jnp.where(kgroup == 1, 0, 2))
    early = (
        jnp.concatenate([projections, mixed], 0),
        qtok[:, None],
        ktok[None, :],
        labels_ext[:, 1][None, :],
        jnp.repeat(offsets, QUERY_ATOMS)[:, None],
        query_term,
        key_term_ext.T,
        band,
        gate,
        own_prod,
        pair_proj.T,
    )
    low1, early = lax.optimization_barrier((low1, early))
    mix, qtok, ktok, valid, offset, cq, ck, band, gate, own_prod, proj_t = early

    low0, low1 = project(low0, w, chunk), project(low1, w, chunk)
    low_left, low_right = (low0[0], low1[0]), (low0[1], low1[1])
    swap = [(0, 1), (1, 0)]
    back = product(low_left, own_right, ch)
    back = (back + lax.ppermute(back, "atm", swap)).astype(jnp.bfloat16)
    main = product(own_left, low_right, ch)
    other = lax.ppermute(main, "atm", swap)
    back = lax.ppermute(back, "tok", down).astype(jnp.float32)
    pair_band, table = tail(own_prod, main, other, back, band, gate, tri_out, proj_t)
    atoms_out = atoms_part(
        mix,
        table,
        qtok,
        ktok,
        valid,
        offset,
        cq,
        ck,
        atom_act,
        atom_cond,
        block_weights,
        groups * lax.axis_size("atm"),
        heads,
    )
    return (pair_band, atoms_out)


def solution(mesh):
    in_specs = (
        P("tok", None, None),
        P(),
        P(),
        P(),
        P(),
        P(("tok", "atm"), None),
        P(("tok", "atm"), None),
        P(),
        P(),
        P(),
        P(),
        P(("tok", "atm")),
        P(("tok", "atm")),
        P(("tok", "atm")),
        P(("tok", "atm"), None),
    )
    out_specs = (P("tok", None, None), P(("tok", "atm"), None))
    return jax.shard_map(local, mesh=mesh, in_specs=in_specs, out_specs=out_specs, check_vma=False)
```

```python
import functools

import jax
import jax.numpy as jnp
from jax import lax
from jax.experimental import pallas as pl
from jax.experimental.pallas import tpu as pltpu
from jax.sharding import PartitionSpec as P

QUERY_ATOMS = 32
KW = 128
HALO = 64
SLOT = 32
LANES = 128
VMEM_LIMIT = 56 * 1024 * 1024
MESH = pl.DeviceIdType.MESH
NT = (((1,), (1,)), ((), ()))
TN = (((0,), (0,)), ((), ()))


def with_halo(x, sides, width):
    for axis, dim in sides:
        peers, length = (lax.axis_size(axis), x.shape[dim])
        up = [(i, (i + 1) % peers) for i in range(peers - 1)]
        down = [(j, i) for i, j in up]
        last = lax.slice_in_dim(x, length - width, length, axis=dim)
        leading = lax.slice_in_dim(x, 0, width, axis=dim)
        before = lax.ppermute(last, axis, up)
        after = lax.ppermute(leading, axis, down)
        x = jnp.concatenate([before, x, after], axis=dim)
    return x


def sigmoid(x):
    return 0.5 * jnp.tanh(0.5 * x) + 0.5


def normalize(values, axis=-1):
    values = values.astype(jnp.float32)
    centred = values - jnp.mean(values, axis, keepdims=True)
    return centred * lax.rsqrt(jnp.mean(centred * centred, axis, keepdims=True) + 1e-05)


def dot(a, b, dims=None):
    if dims is None:
        return jnp.dot(a, b, preferred_element_type=jnp.float32)
    return lax.dot_general(a, b, dims, preferred_element_type=jnp.float32)


def project_kernel(rows, chunk, lane_tiles, x_ref, w_ref, a_ref, b_ref, a_acc, b_acc):
    step = pl.program_id(1)
    ch = w_ref.shape[0] // 4
    for r in range(rows):
        zn = normalize(x_ref[r]).astype(jnp.bfloat16)
        pad = lane_tiles * LANES - chunk
        if pad:
            zn = jnp.concatenate([zn, jnp.zeros((pad, zn.shape[1]), zn.dtype)], axis=0)
        parts = dot(w_ref[...], zn, NT)
        left = sigmoid(parts[0:ch]) * parts[ch : 2 * ch]
        right = sigmoid(parts[2 * ch : 3 * ch]) * parts[3 * ch : 4 * ch]
        row = step * rows + r
        for q in range(lane_tiles):
            cols = slice(q * LANES, (q + 1) * LANES)
            a_acc[q, pl.ds(row, ch, stride=SLOT), :] = left[:, cols]
            b_acc[q, pl.ds(row, ch, stride=SLOT), :] = right[:, cols]

    @pl.when(step == pl.num_programs(1) - 1)
    def _():
        a_ref[0] = a_acc[...].astype(jnp.bfloat16)
        b_ref[0] = b_acc[...].astype(jnp.bfloat16)


def project(x, w, chunk):
    part, span, width = x.shape
    ch = w.shape[0] // 4
    rows = part // 4
    tiles = -(-chunk // LANES)
    shape = (tiles, ch * SLOT, LANES)
    out = jax.ShapeDtypeStruct((span // chunk,) + shape, jnp.bfloat16)
    out_spec = pl.BlockSpec((1,) + shape, lambda k, i: (k, 0, 0, 0))
    return pl.pallas_call(
        functools.partial(project_kernel, rows, chunk, tiles),
        grid=(span // chunk, part // rows),
        in_specs=[
            pl.BlockSpec((rows, chunk, width), lambda k, i: (i, k, 0)),
            pl.BlockSpec(w.shape, lambda k, i: (0, 0)),
        ],
        out_specs=[out_spec, out_spec],
        out_shape=[out, out],
        scratch_shapes=[pltpu.VMEM(shape, jnp.float32)] * 2,
        compiler_params=pltpu.CompilerParams(vmem_limit_bytes=VMEM_LIMIT),
        cost_estimate=pl.CostEstimate(
            flops=2 * x.size * 4 * ch, bytes_accessed=16 * x.size, transcendentals=2 * x.size
        ),
        name="project",
    )(x, w)


def product_kernel(ch, a_ref, b_ref, out_ref):
    quarter = ch // 4
    tiles = a_ref.shape[1]

    @pl.when(pl.program_id(0) == 0)
    def _():
        out_ref[...] = jnp.zeros_like(out_ref)

    def load(ref, at):
        return jnp.concatenate([ref[0, q, pl.ds(at, SLOT), :] for q in range(tiles)], axis=1)

    def group(g, carry):
        outs = []
        for cl in range(4):
            at = pl.multiple_of((cl * quarter + g) * SLOT, SLOT)
            outs.append(dot(load(a_ref, at), load(b_ref, at), NT))
        out_ref[pl.ds(pl.multiple_of(g * SLOT, SLOT), SLOT), :] += jnp.concatenate(outs, axis=1)
        return carry

    lax.fori_loop(0, quarter, group, 0, unroll=4)


def product(left, right, ch):
    chunks, tiles, rows, lanes = left.shape
    spec = pl.BlockSpec((1, tiles, rows, lanes), lambda k: (k, 0, 0, 0))
    out_rows = ch // 4 * SLOT
    return pl.pallas_call(
        functools.partial(product_kernel, ch),
        grid=(chunks,),
        in_specs=[spec] * 2,
        out_specs=pl.BlockSpec((out_rows, LANES), lambda k: (0, 0)),
        out_shape=jax.ShapeDtypeStruct((out_rows, LANES), jnp.float32),
        compiler_params=pltpu.CompilerParams(vmem_limit_bytes=VMEM_LIMIT),
        cost_estimate=pl.CostEstimate(
            flops=2 * SLOT * SLOT * ch * chunks * tiles * lanes,
            bytes_accessed=16 * chunks * tiles * rows * lanes,
            transcendentals=0,
        ),
        name="product",
    )(left, right)


def gate_kernel(band_ref, gate_ref, out_ref):
    rows, width, c = band_ref.shape
    band = band_ref[...].reshape(rows * width, c)
    gate = sigmoid(dot(normalize(band).astype(jnp.bfloat16), gate_ref[...]))
    out_ref[...] = gate.reshape(rows, width, c)


def gates_of(band, tri_gate):
    tok_dev, width, c = band.shape
    rows = tok_dev // 4
    spec = pl.BlockSpec((rows, width, c), lambda i: (i, 0, 0))
    return pl.pallas_call(
        gate_kernel,
        grid=(tok_dev // rows,),
        in_specs=[spec, pl.BlockSpec(tri_gate.shape, lambda i: (0, 0))],
        out_specs=spec,
        out_shape=jax.ShapeDtypeStruct(band.shape, jnp.float32),
        compiler_params=pltpu.CompilerParams(vmem_limit_bytes=VMEM_LIMIT),
        cost_estimate=pl.CostEstimate(
            flops=2 * band.size * c, bytes_accessed=16 * band.size, transcendentals=band.size
        ),
        name="gate",
    )(band, tri_gate)


def tail_kernel(rows, tok_dev, ch, o1_ref, o2_ref, m1_ref, m2_ref, d_ref, band_ref, gate_ref, out_w_ref,
                proj_ref, band_out_ref, table_ref):
    step = pl.program_id(0)
    quarter = ch // 4
    cp = proj_ref.shape[0]
    width, c = band_ref.shape[1:]

    @pl.when(step == 0)
    def _():
        table_ref[...] = jnp.zeros_like(table_ref)

    places, updates = [], []
    for r in range(rows):
        row = step * rows + r
        places.append(row)
        near = pl.ds(row, quarter, stride=SLOT)
        packed = [
            o1_ref[near, :] + o2_ref[near, :],
            m1_ref[near, :] + m2_ref[near, :],
            d_ref[near, :].astype(jnp.float32),
        ]
        prod = jnp.concatenate(
            [
                jnp.concatenate([p[:, q * SLOT : (q + 1) * SLOT] for p in packed], axis=1)
                for q in range(4)
            ],
            axis=0,
        )
        pn = normalize(prod, 0).astype(jnp.bfloat16)
        updates.append(dot(pn, out_w_ref[...], TN))
    band = band_ref[...].reshape(rows * width, c).astype(jnp.float32)
    gate = gate_ref[...].reshape(rows * width, c)
    new = (band + gate * jnp.concatenate(updates, axis=0)).astype(jnp.bfloat16)
    zt = normalize(new).astype(jnp.bfloat16)
    lane = lax.broadcasted_iota(jnp.int32, (cp, width), 1)
    used = lax.rem(lane, SLOT) < tok_dev
    plain = new.astype(jnp.float32)
    for r in range(rows):
        pieces = []
        for slot in (1, 0, 2):
            at = r * width + slot * SLOT
            pieces.append(plain[at : at + tok_dev])
        band_out_ref[r] = jnp.concatenate(pieces, axis=0).astype(jnp.bfloat16)
        tok = dot(proj_ref[...], zt[r * width : (r + 1) * width], NT)
        tok = jnp.where(used, tok, 0.0)
        tok = jnp.concatenate([tok, jnp.zeros((cp, LANES - width), jnp.float32)], axis=1)
        table_ref[pl.ds(places[r], cp, stride=SLOT), :] = tok


def tail(o1, o2, m1, m2, d, band, gate, tri_out, proj_t):
    tok_dev, width, c = band.shape
    ch = tri_out.shape[0]
    cp = proj_t.shape[0]
    rows = 4
    whole = lambda x: pl.BlockSpec(x.shape, lambda i: (0, 0))
    band_spec = pl.BlockSpec((rows, width, c), lambda i: (i, 0, 0))
    return pl.pallas_call(
        functools.partial(tail_kernel, rows, tok_dev, ch),
        grid=(tok_dev // rows,),
        in_specs=[whole(o1), whole(o2), whole(m1), whole(m2), whole(d), band_spec, band_spec,
                  whole(tri_out), whole(proj_t)],
        out_specs=[
            pl.BlockSpec((rows, 3 * tok_dev, c), lambda i: (i, 0, 0)),
            pl.BlockSpec((cp * SLOT, LANES), lambda i: (0, 0)),
        ],
        out_shape=[
            jax.ShapeDtypeStruct((tok_dev, 3 * tok_dev, c), jnp.bfloat16),
            jax.ShapeDtypeStruct((cp * SLOT, LANES), jnp.float32),
        ],
        compiler_params=pltpu.CompilerParams(vmem_limit_bytes=VMEM_LIMIT),
        name="tail",
    )(o1, o2, m1, m2, d, band, gate, tri_out, proj_t)


def atom_kernel(devices, heads, blocks, tok_dev, mix_ref, table_ref, q_ref, k_ref, act_ref, cond_ref, w_ref, out_ref,
                ext, bias, planes, send_sem, recv_sem):
    atoms, width = act_ref.shape
    span = atoms + 2 * HALO
    cp = k_ref.shape[0] - 2
    head_dim = width // heads
    me = lax.axis_index("tok") * 2 + lax.axis_index("atm")
    above, below = me + 1, me - 1
    has_above, has_below = me < devices - 1, me > 0

    def place(d):
        d = jnp.clip(d, 0, devices - 1)
        return (d // 2, d % 2)

    barrier = pltpu.get_barrier_semaphore()

    @pl.when(has_below)
    def _():
        pl.semaphore_signal(barrier, inc=1, device_id=place(below), device_id_type=MESH)

    @pl.when(has_above)
    def _():
        pl.semaphore_signal(barrier, inc=1, device_id=place(above), device_id_type=MESH)

    def copies(b):
        up = pltpu.make_async_remote_copy(
            src_ref=ext.at[b, pl.ds(atoms, HALO)],
            dst_ref=ext.at[b, pl.ds(0, HALO)],
            send_sem=send_sem.at[b, 0],
            recv_sem=recv_sem.at[b, 0],
            device_id=place(above),
            device_id_type=MESH,
        )
        down = pltpu.make_async_remote_copy(
            src_ref=ext.at[b, pl.ds(HALO, HALO)],
            dst_ref=ext.at[b, pl.ds(HALO + atoms, HALO)],
            send_sem=send_sem.at[b, 1],
            recv_sem=recv_sem.at[b, 1],
            device_id=place(below),
            device_id_type=MESH,
        )
        return up, down

    @pl.when(jnp.logical_not(has_below))
    def _():
        for b in range(blocks):
            ext[b, pl.ds(0, HALO)] = jnp.zeros((HALO, width), jnp.bfloat16)

    @pl.when(jnp.logical_not(has_above))
    def _():
        for b in range(blocks):
            ext[b, pl.ds(HALO + atoms, HALO)] = jnp.zeros((HALO, width), jnp.bfloat16)

    cond = normalize(cond_ref[...]).astype(jnp.bfloat16)
    state = act_ref[...].astype(jnp.float32)
    scales = [sigmoid(dot(cond, w_ref[b, 0])) for b in range(blocks)]
    shifts = [dot(cond, w_ref[b, 1]) for b in range(blocks)]

    def begin(b, state):
        normed = (scales[b] * normalize(state) + shifts[b]).astype(jnp.bfloat16)
        ext[b, pl.ds(HALO, atoms)] = normed
        if b == 0:

            @pl.when(jnp.logical_and(has_below, has_above))
            def _():
                pl.semaphore_wait(barrier, 2)

            @pl.when(jnp.logical_not(jnp.logical_and(has_below, has_above)))
            def _():
                pl.semaphore_wait(barrier, 1)

        up, down = copies(b)

        @pl.when(has_above)
        def _():
            up.start()

        @pl.when(has_below)
        def _():
            down.start()

        return normed

    def finish(b):
        up, down = copies(b)

        @pl.when(has_above)
        def _():
            up.wait_send()
            down.wait_recv()

        @pl.when(has_below)
        def _():
            down.wait_send()
            up.wait_recv()

    normed = begin(0, state)

    shard = lax.axis_index("tok")
    qtok = q_ref[:, cp : cp + 1].astype(jnp.int32) - shard * tok_dev
    ktok = k_ref[cp : cp + 1, :].astype(jnp.int32) - (shard - 1) * tok_dev
    ktok = jnp.where(
        ktok < tok_dev,
        ktok + SLOT,
        jnp.where(ktok < 2 * tok_dev, ktok - tok_dev, ktok + 2 * (SLOT - tok_dev)),
    )
    qhot = (qtok == lax.broadcasted_iota(jnp.int32, (atoms, SLOT), 1)).astype(jnp.float32)
    qhot = qhot.astype(jnp.bfloat16)
    khot = (ktok == lax.broadcasted_iota(jnp.int32, (LANES, span), 0)).astype(jnp.float32)
    khot = khot.astype(jnp.bfloat16)
    picked = dot(table_ref[...].astype(jnp.bfloat16), khot).astype(jnp.bfloat16)
    for c in range(cp):
        sel = dot(qhot, picked[c * SLOT : (c + 1) * SLOT])
        planes[c] = sel + q_ref[:, c : c + 1] + k_ref[c : c + 1, :]
    key = lax.broadcasted_iota(jnp.int32, (atoms, span), 1)
    begin_key = q_ref[:, cp + 1 : cp + 2].astype(jnp.int32)
    live = jnp.logical_and(key >= begin_key, key < begin_key + KW)
    live = jnp.logical_and(live, k_ref[cp + 1 : cp + 2, :] > 0.5)
    outs = blocks * heads
    rows = 16

    def mix(g, carry):
        at = pl.ds(pl.multiple_of(g * rows, rows), rows)
        total = [None] * outs
        for c in range(cp):
            base = planes[c, at, :]
            positive = jnp.maximum(base, 0.0)
            for o in range(outs):
                term = base * mix_ref[c, o] + positive * mix_ref[cp + c, o]
                total[o] = term if c == 0 else total[o] + term
        for o in range(outs):
            bias[o, at, :] = total[o]
        return carry

    lax.fori_loop(0, atoms // rows, mix, 0)

    for b in range(blocks):
        if b:
            normed = begin(b, state)
        queries = (dot(normed, w_ref[b, 2]) * head_dim**-0.5).astype(jnp.bfloat16)
        gates = sigmoid(dot(normed, w_ref[b, 5]))
        finish(b)
        full = ext[b]
        keys = dot(full, w_ref[b, 3]).astype(jnp.bfloat16)
        values = dot(full, w_ref[b, 4]).astype(jnp.bfloat16)
        blended = []
        for h in range(heads):
            cols = slice(h * head_dim, (h + 1) * head_dim)
            logits = dot(queries[:, cols], keys[:, cols], NT) + bias[b * heads + h]
            logits = jnp.where(live, logits, -1e30)
            weights = jnp.exp(logits - jnp.max(logits, -1, keepdims=True))
            probs = (weights / jnp.sum(weights, -1, keepdims=True)).astype(jnp.bfloat16)
            blended.append(dot(probs, values[:, cols]))
        attended = (jnp.concatenate(blended, axis=1) * gates).astype(jnp.bfloat16)
        state = state + dot(attended, w_ref[b, 6])
    out_ref[...] = state.astype(jnp.bfloat16)


def atoms_part(mix, table, q, k, act, cond, weights, devices, heads, tok_dev):
    atoms, width = act.shape
    span = atoms + 2 * HALO
    blocks = weights.shape[0]
    vmem = pl.BlockSpec(memory_space=pltpu.VMEM)
    return pl.pallas_call(
        functools.partial(atom_kernel, devices, heads, blocks, tok_dev),
        in_specs=[pl.BlockSpec(memory_space=pltpu.SMEM)] + [vmem] * 6,
        out_specs=vmem,
        out_shape=jax.ShapeDtypeStruct(act.shape, jnp.bfloat16),
        scratch_shapes=[
            pltpu.VMEM((blocks, span, width), jnp.bfloat16),
            pltpu.VMEM((blocks * heads, atoms, span), jnp.float32),
            pltpu.VMEM((k.shape[0] - 2, atoms, span), jnp.float32),
            pltpu.SemaphoreType.DMA((blocks, 2)),
            pltpu.SemaphoreType.DMA((blocks, 2)),
        ],
        compiler_params=pltpu.CompilerParams(
            collective_id=0, has_side_effects=True, vmem_limit_bytes=VMEM_LIMIT
        ),
        name="atoms",
    )(mix, table, q, k, act, cond, weights)


def local(
    pair,
    tri_in,
    tri_gate,
    tri_out,
    pair_proj,
    atom_act,
    atom_cond,
    cond_pair,
    pair_mlp,
    bias_proj,
    block_weights,
    atom_token,
    atom_mask,
    key_start,
    key_tiles,
):
    tok_dev, tokens, _ = pair.shape
    groups = lax.axis_size("tok")
    ch = tri_in.shape[2]
    shard = lax.axis_index("tok")
    core = lax.axis_index("atm")
    up = [(i, i + 1) for i in range(groups - 1)]
    down = [(i + 1, i) for i in range(groups - 1)]

    half = tokens // 2
    chunk = 8 * tok_dev
    swap = [(0, 1), (1, 0)]
    own = lax.dynamic_slice_in_dim(pair, core * half, half, 1)
    low = lax.ppermute(own, "tok", up)
    w = jnp.swapaxes(tri_in, 1, 2).reshape(4 * ch, -1)
    own_left, own_right = project(own, w, chunk)
    own_prod = product(own_left, own_right, ch)
    own_other = lax.ppermute(own_prod, "atm", swap)

    padded = jnp.pad(pair, ((0, 0), (tok_dev, tok_dev), (0, 0)))
    band = lax.dynamic_slice_in_dim(padded, shard * tok_dev, 3 * tok_dev, 1)
    band = band.reshape(tok_dev, 3, tok_dev, -1)
    band = jnp.concatenate([band[:, 1:2], band[:, 0:1], band[:, 2:3]], axis=1)
    band = jnp.pad(band, ((0, 0), (0, 0), (0, SLOT - tok_dev), (0, 0)))
    band = band.reshape(tok_dev, 3 * SLOT, -1)
    gate = gates_of(band, tri_gate)

    atoms = atom_act.shape[0]
    heads = bias_proj.shape[2]
    device = shard * lax.axis_size("atm") + core
    labels = jnp.stack([atom_token, atom_mask], 1).astype(jnp.float32)
    relu_cond = jax.nn.relu(atom_cond)
    query_term = jnp.dot(relu_cond, cond_pair[0], preferred_element_type=jnp.float32)
    key_term = jnp.dot(relu_cond, cond_pair[1], preferred_element_type=jnp.float32)
    keys = jnp.concatenate([key_term, labels], 1)
    keys = with_halo(keys, ((("tok", "atm"), 0),), HALO).T
    offsets = key_start - device * atoms + HALO
    projections = jnp.swapaxes(bias_proj, 0, 1).reshape(bias_proj.shape[1], -1).astype(jnp.float32)
    mixed = jnp.dot(
        pair_mlp.astype(jnp.float32), projections, precision=lax.Precision.HIGHEST
    )
    starts = jnp.repeat(offsets, QUERY_ATOMS).astype(jnp.float32)
    queries = jnp.concatenate([query_term, labels[:, :1], starts[:, None]], 1)
    mix = jnp.concatenate([projections, mixed], 0)
    early = (mix, queries, keys, band, gate, own_prod, own_other, pair_proj.T)
    low, early = lax.optimization_barrier((low, early))
    mix, queries, keys, band, gate, own_prod, own_other, proj_t = early

    low_left, low_right = project(low, w, chunk)
    back = product(low_left, own_right, ch)
    back = (back + lax.ppermute(back, "atm", swap)).astype(jnp.bfloat16)
    main = product(own_left, low_right, ch)
    other = lax.ppermute(main, "atm", swap)
    back = lax.ppermute(back, "tok", down).astype(jnp.float32)
    pair_band, table = tail(own_prod, own_other, main, other, back, band, gate, tri_out, proj_t)
    atoms_out = atoms_part(
        mix,
        table,
        queries,
        keys,
        atom_act,
        atom_cond,
        block_weights,
        groups * lax.axis_size("atm"),
        heads,
        tok_dev,
    )
    return (pair_band, atoms_out)


def solution(mesh):
    in_specs = (
        P("tok", None, None),
        P(),
        P(),
        P(),
        P(),
        P(("tok", "atm"), None),
        P(("tok", "atm"), None),
        P(),
        P(),
        P(),
        P(),
        P(("tok", "atm")),
        P(("tok", "atm")),
        P(("tok", "atm")),
        P(("tok", "atm"), None),
    )
    out_specs = (P("tok", None, None), P(("tok", "atm"), None))
    return jax.shard_map(local, mesh=mesh, in_specs=in_specs, out_specs=out_specs, check_vma=False)
```

```python
import functools

import jax
import jax.numpy as jnp
from jax import lax
from jax.experimental import pallas as pl
from jax.experimental.pallas import tpu as pltpu
from jax.sharding import PartitionSpec as P

QUERY_ATOMS = 32
KW = 128
HALO = 64
SLOT = 32
LANES = 128
VMEM_LIMIT = 56 * 1024 * 1024
MESH = pl.DeviceIdType.MESH
NT = (((1,), (1,)), ((), ()))
TN = (((0,), (0,)), ((), ()))


def with_halo(x, sides, width):
    for axis, dim in sides:
        peers, length = (lax.axis_size(axis), x.shape[dim])
        up = [(i, (i + 1) % peers) for i in range(peers - 1)]
        down = [(j, i) for i, j in up]
        last = lax.slice_in_dim(x, length - width, length, axis=dim)
        leading = lax.slice_in_dim(x, 0, width, axis=dim)
        before = lax.ppermute(last, axis, up)
        after = lax.ppermute(leading, axis, down)
        x = jnp.concatenate([before, x, after], axis=dim)
    return x


def sigmoid(x):
    return 0.5 * jnp.tanh(0.5 * x) + 0.5


def normalize(values, axis=-1):
    values = values.astype(jnp.float32)
    centred = values - jnp.mean(values, axis, keepdims=True)
    return centred * lax.rsqrt(jnp.mean(centred * centred, axis, keepdims=True) + 1e-05)


def dot(a, b, dims=None):
    if dims is None:
        return jnp.dot(a, b, preferred_element_type=jnp.float32)
    return lax.dot_general(a, b, dims, preferred_element_type=jnp.float32)


def project_kernel(rows, chunk, lane_tiles, x_ref, w_ref, a_ref, b_ref, a_acc, b_acc):
    step = pl.program_id(1)
    ch = w_ref.shape[0] // 4
    for r in range(rows):
        zn = normalize(x_ref[r]).astype(jnp.bfloat16)
        pad = lane_tiles * LANES - chunk
        if pad:
            zn = jnp.concatenate([zn, jnp.zeros((pad, zn.shape[1]), zn.dtype)], axis=0)
        parts = dot(w_ref[...], zn, NT)
        left = sigmoid(parts[0:ch]) * parts[ch : 2 * ch]
        right = sigmoid(parts[2 * ch : 3 * ch]) * parts[3 * ch : 4 * ch]
        row = step * rows + r
        for q in range(lane_tiles):
            cols = slice(q * LANES, (q + 1) * LANES)
            a_acc[q, pl.ds(row, ch, stride=SLOT), :] = left[:, cols]
            b_acc[q, pl.ds(row, ch, stride=SLOT), :] = right[:, cols]

    @pl.when(step == pl.num_programs(1) - 1)
    def _():
        a_ref[0] = a_acc[...].astype(jnp.bfloat16)
        b_ref[0] = b_acc[...].astype(jnp.bfloat16)


def project(x, w, chunk):
    part, span, width = x.shape
    ch = w.shape[0] // 4
    rows = part // 4
    tiles = -(-chunk // LANES)
    shape = (tiles, ch * SLOT, LANES)
    out = jax.ShapeDtypeStruct((span // chunk,) + shape, jnp.bfloat16)
    out_spec = pl.BlockSpec((1,) + shape, lambda k, i: (k, 0, 0, 0))
    return pl.pallas_call(
        functools.partial(project_kernel, rows, chunk, tiles),
        grid=(span // chunk, part // rows),
        in_specs=[
            pl.BlockSpec((rows, chunk, width), lambda k, i: (i, k, 0)),
            pl.BlockSpec(w.shape, lambda k, i: (0, 0)),
        ],
        out_specs=[out_spec, out_spec],
        out_shape=[out, out],
        scratch_shapes=[pltpu.VMEM(shape, jnp.float32)] * 2,
        compiler_params=pltpu.CompilerParams(vmem_limit_bytes=VMEM_LIMIT),
        cost_estimate=pl.CostEstimate(
            flops=2 * x.size * 4 * ch, bytes_accessed=16 * x.size, transcendentals=2 * x.size
        ),
        name="project",
    )(x, w)


def product_kernel(ch, a_ref, b_ref, out_ref):
    quarter = ch // 4
    tiles = a_ref.shape[1]

    @pl.when(pl.program_id(0) == 0)
    def _():
        out_ref[...] = jnp.zeros_like(out_ref)

    def load(ref, at):
        return jnp.concatenate([ref[0, q, pl.ds(at, SLOT), :] for q in range(tiles)], axis=1)

    def group(g, carry):
        outs = []
        for cl in range(4):
            at = pl.multiple_of((cl * quarter + g) * SLOT, SLOT)
            outs.append(dot(load(a_ref, at), load(b_ref, at), NT))
        out_ref[pl.ds(pl.multiple_of(g * SLOT, SLOT), SLOT), :] += jnp.concatenate(outs, axis=1)
        return carry

    lax.fori_loop(0, quarter, group, 0, unroll=4)


def product(left, right, ch):
    chunks, tiles, rows, lanes = left.shape
    spec = pl.BlockSpec((1, tiles, rows, lanes), lambda k: (k, 0, 0, 0))
    out_rows = ch // 4 * SLOT
    return pl.pallas_call(
        functools.partial(product_kernel, ch),
        grid=(chunks,),
        in_specs=[spec] * 2,
        out_specs=pl.BlockSpec((out_rows, LANES), lambda k: (0, 0)),
        out_shape=jax.ShapeDtypeStruct((out_rows, LANES), jnp.float32),
        compiler_params=pltpu.CompilerParams(vmem_limit_bytes=VMEM_LIMIT),
        cost_estimate=pl.CostEstimate(
            flops=2 * SLOT * SLOT * ch * chunks * tiles * lanes,
            bytes_accessed=16 * chunks * tiles * rows * lanes,
            transcendentals=0,
        ),
        name="product",
    )(left, right)


def gate_kernel(band_ref, gate_ref, out_ref):
    rows, width, c = band_ref.shape
    band = band_ref[...].reshape(rows * width, c)
    gate = sigmoid(dot(normalize(band).astype(jnp.bfloat16), gate_ref[...]))
    out_ref[...] = gate.reshape(rows, width, c)


def gates_of(band, tri_gate):
    tok_dev, width, c = band.shape
    rows = tok_dev // 4
    spec = pl.BlockSpec((rows, width, c), lambda i: (i, 0, 0))
    return pl.pallas_call(
        gate_kernel,
        grid=(tok_dev // rows,),
        in_specs=[spec, pl.BlockSpec(tri_gate.shape, lambda i: (0, 0))],
        out_specs=spec,
        out_shape=jax.ShapeDtypeStruct(band.shape, jnp.float32),
        compiler_params=pltpu.CompilerParams(vmem_limit_bytes=VMEM_LIMIT),
        cost_estimate=pl.CostEstimate(
            flops=2 * band.size * c, bytes_accessed=16 * band.size, transcendentals=band.size
        ),
        name="gate",
    )(band, tri_gate)


def tail_kernel(rows, tok_dev, ch, o1_ref, o2_ref, m1_ref, m2_ref, d_ref, band_ref, gate_ref, out_w_ref,
                proj_ref, band_out_ref, table_ref):
    step = pl.program_id(0)
    quarter = ch // 4
    cp = proj_ref.shape[0]
    width, c = band_ref.shape[1:]

    @pl.when(step == 0)
    def _():
        table_ref[...] = jnp.zeros_like(table_ref)

    places, updates = [], []
    for r in range(rows):
        row = step * rows + r
        places.append(row)
        near = pl.ds(row, quarter, stride=SLOT)
        packed = [
            o1_ref[near, :] + o2_ref[near, :],
            m1_ref[near, :] + m2_ref[near, :],
            d_ref[near, :].astype(jnp.float32),
        ]
        prod = jnp.concatenate(
            [
                jnp.concatenate([p[:, q * SLOT : (q + 1) * SLOT] for p in packed], axis=1)
                for q in range(4)
            ],
            axis=0,
        )
        pn = normalize(prod, 0).astype(jnp.bfloat16)
        updates.append(dot(pn, out_w_ref[...], TN))
    band = band_ref[...].reshape(rows * width, c).astype(jnp.float32)
    gate = gate_ref[...].reshape(rows * width, c)
    new = (band + gate * jnp.concatenate(updates, axis=0)).astype(jnp.bfloat16)
    zt = normalize(new).astype(jnp.bfloat16)
    lane = lax.broadcasted_iota(jnp.int32, (cp, width), 1)
    used = lax.rem(lane, SLOT) < tok_dev
    plain = new.astype(jnp.float32)
    for r in range(rows):
        pieces = []
        for slot in (1, 0, 2):
            at = r * width + slot * SLOT
            pieces.append(plain[at : at + tok_dev])
        band_out_ref[r] = jnp.concatenate(pieces, axis=0).astype(jnp.bfloat16)
        tok = dot(proj_ref[...], zt[r * width : (r + 1) * width], NT)
        tok = jnp.where(used, tok, 0.0)
        tok = jnp.concatenate([tok, jnp.zeros((cp, LANES - width), jnp.float32)], axis=1)
        table_ref[pl.ds(places[r], cp, stride=SLOT), :] = tok


def tail(o1, o2, m1, m2, d, band, gate, tri_out, proj_t):
    tok_dev, width, c = band.shape
    ch = tri_out.shape[0]
    cp = proj_t.shape[0]
    rows = tok_dev // 4
    whole = lambda x: pl.BlockSpec(x.shape, lambda i: (0, 0))
    band_spec = pl.BlockSpec((rows, width, c), lambda i: (i, 0, 0))
    return pl.pallas_call(
        functools.partial(tail_kernel, rows, tok_dev, ch),
        grid=(tok_dev // rows,),
        in_specs=[whole(o1), whole(o2), whole(m1), whole(m2), whole(d), band_spec, band_spec,
                  whole(tri_out), whole(proj_t)],
        out_specs=[
            pl.BlockSpec((rows, 3 * tok_dev, c), lambda i: (i, 0, 0)),
            pl.BlockSpec((cp * SLOT, LANES), lambda i: (0, 0)),
        ],
        out_shape=[
            jax.ShapeDtypeStruct((tok_dev, 3 * tok_dev, c), jnp.bfloat16),
            jax.ShapeDtypeStruct((cp * SLOT, LANES), jnp.float32),
        ],
        compiler_params=pltpu.CompilerParams(vmem_limit_bytes=VMEM_LIMIT),
        name="tail",
    )(o1, o2, m1, m2, d, band, gate, tri_out, proj_t)


def atom_kernel(devices, heads, blocks, tok_dev, mix_ref, table_ref, q_ref, k_ref, act_ref, cond_ref, w_ref, out_ref,
                ext, bias, planes, send_sem, recv_sem):
    atoms, width = act_ref.shape
    span = atoms + 2 * HALO
    cp = k_ref.shape[0] - 2
    head_dim = width // heads
    me = lax.axis_index("tok") * 2 + lax.axis_index("atm")
    above, below = me + 1, me - 1
    has_above, has_below = me < devices - 1, me > 0

    def place(d):
        d = jnp.clip(d, 0, devices - 1)
        return (d // 2, d % 2)

    barrier = pltpu.get_barrier_semaphore()

    @pl.when(has_below)
    def _():
        pl.semaphore_signal(barrier, inc=1, device_id=place(below), device_id_type=MESH)

    @pl.when(has_above)
    def _():
        pl.semaphore_signal(barrier, inc=1, device_id=place(above), device_id_type=MESH)

    def copies(b):
        up = pltpu.make_async_remote_copy(
            src_ref=ext.at[b, pl.ds(atoms, HALO)],
            dst_ref=ext.at[b, pl.ds(0, HALO)],
            send_sem=send_sem.at[b, 0],
            recv_sem=recv_sem.at[b, 0],
            device_id=place(above),
            device_id_type=MESH,
        )
        down = pltpu.make_async_remote_copy(
            src_ref=ext.at[b, pl.ds(HALO, HALO)],
            dst_ref=ext.at[b, pl.ds(HALO + atoms, HALO)],
            send_sem=send_sem.at[b, 1],
            recv_sem=recv_sem.at[b, 1],
            device_id=place(below),
            device_id_type=MESH,
        )
        return up, down

    @pl.when(jnp.logical_not(has_below))
    def _():
        for b in range(blocks):
            ext[b, pl.ds(0, HALO)] = jnp.zeros((HALO, width), jnp.bfloat16)

    @pl.when(jnp.logical_not(has_above))
    def _():
        for b in range(blocks):
            ext[b, pl.ds(HALO + atoms, HALO)] = jnp.zeros((HALO, width), jnp.bfloat16)

    cond = normalize(cond_ref[...]).astype(jnp.bfloat16)
    state = act_ref[...].astype(jnp.float32)
    scales = [sigmoid(dot(cond, w_ref[b, 0])) for b in range(blocks)]
    shifts = [dot(cond, w_ref[b, 1]) for b in range(blocks)]

    def begin(b, state):
        normed = (scales[b] * normalize(state) + shifts[b]).astype(jnp.bfloat16)
        ext[b, pl.ds(HALO, atoms)] = normed
        if b == 0:

            @pl.when(jnp.logical_and(has_below, has_above))
            def _():
                pl.semaphore_wait(barrier, 2)

            @pl.when(jnp.logical_not(jnp.logical_and(has_below, has_above)))
            def _():
                pl.semaphore_wait(barrier, 1)

        up, down = copies(b)

        @pl.when(has_above)
        def _():
            up.start()

        @pl.when(has_below)
        def _():
            down.start()

        return normed

    def finish(b):
        up, down = copies(b)

        @pl.when(has_above)
        def _():
            up.wait_send()
            down.wait_recv()

        @pl.when(has_below)
        def _():
            down.wait_send()
            up.wait_recv()

    normed = begin(0, state)

    shard = lax.axis_index("tok")
    qtok = q_ref[:, cp : cp + 1].astype(jnp.int32) - shard * tok_dev
    ktok = k_ref[cp : cp + 1, :].astype(jnp.int32) - (shard - 1) * tok_dev
    ktok = jnp.where(
        ktok < tok_dev,
        ktok + SLOT,
        jnp.where(ktok < 2 * tok_dev, ktok - tok_dev, ktok + 2 * (SLOT - tok_dev)),
    )
    qhot = (qtok == lax.broadcasted_iota(jnp.int32, (atoms, SLOT), 1)).astype(jnp.float32)
    qhot = qhot.astype(jnp.bfloat16)
    khot = (ktok == lax.broadcasted_iota(jnp.int32, (LANES, span), 0)).astype(jnp.float32)
    khot = khot.astype(jnp.bfloat16)
    picked = dot(table_ref[...].astype(jnp.bfloat16), khot).astype(jnp.bfloat16)
    for c in range(cp):
        sel = dot(qhot, picked[c * SLOT : (c + 1) * SLOT])
        planes[c] = sel + q_ref[:, c : c + 1] + k_ref[c : c + 1, :]
    key = lax.broadcasted_iota(jnp.int32, (atoms, span), 1)
    begin_key = q_ref[:, cp + 1 : cp + 2].astype(jnp.int32)
    live = jnp.logical_and(key >= begin_key, key < begin_key + KW)
    live = jnp.logical_and(live, k_ref[cp + 1 : cp + 2, :] > 0.5)
    outs = blocks * heads
    rows = 16

    def mix(g, carry):
        at = pl.ds(pl.multiple_of(g * rows, rows), rows)
        total = [None] * outs
        for c in range(cp):
            base = planes[c, at, :]
            positive = jnp.maximum(base, 0.0)
            for o in range(outs):
                term = base * mix_ref[c, o] + positive * mix_ref[cp + c, o]
                total[o] = term if c == 0 else total[o] + term
        for o in range(outs):
            bias[o, at, :] = total[o]
        return carry

    lax.fori_loop(0, atoms // rows, mix, 0)

    for b in range(blocks):
        if b:
            normed = begin(b, state)
        queries = (dot(normed, w_ref[b, 2]) * head_dim**-0.5).astype(jnp.bfloat16)
        gates = sigmoid(dot(normed, w_ref[b, 5]))
        finish(b)
        full = ext[b]
        keys = dot(full, w_ref[b, 3]).astype(jnp.bfloat16)
        values = dot(full, w_ref[b, 4]).astype(jnp.bfloat16)
        blended = []
        for h in range(heads):
            cols = slice(h * head_dim, (h + 1) * head_dim)
            logits = dot(queries[:, cols], keys[:, cols], NT) + bias[b * heads + h]
            logits = jnp.where(live, logits, -1e30)
            weights = jnp.exp(logits - jnp.max(logits, -1, keepdims=True))
            probs = (weights / jnp.sum(weights, -1, keepdims=True)).astype(jnp.bfloat16)
            blended.append(dot(probs, values[:, cols]))
        attended = (jnp.concatenate(blended, axis=1) * gates).astype(jnp.bfloat16)
        state = state + dot(attended, w_ref[b, 6])
    out_ref[...] = state.astype(jnp.bfloat16)


def atoms_part(mix, table, q, k, act, cond, weights, devices, heads, tok_dev):
    atoms, width = act.shape
    span = atoms + 2 * HALO
    blocks = weights.shape[0]
    vmem = pl.BlockSpec(memory_space=pltpu.VMEM)
    return pl.pallas_call(
        functools.partial(atom_kernel, devices, heads, blocks, tok_dev),
        in_specs=[pl.BlockSpec(memory_space=pltpu.SMEM)] + [vmem] * 6,
        out_specs=vmem,
        out_shape=jax.ShapeDtypeStruct(act.shape, jnp.bfloat16),
        scratch_shapes=[
            pltpu.VMEM((blocks, span, width), jnp.bfloat16),
            pltpu.VMEM((blocks * heads, atoms, span), jnp.float32),
            pltpu.VMEM((k.shape[0] - 2, atoms, span), jnp.float32),
            pltpu.SemaphoreType.DMA((blocks, 2)),
            pltpu.SemaphoreType.DMA((blocks, 2)),
        ],
        compiler_params=pltpu.CompilerParams(
            collective_id=0, has_side_effects=True, vmem_limit_bytes=VMEM_LIMIT
        ),
        name="atoms",
    )(mix, table, q, k, act, cond, weights)


def local(
    pair,
    tri_in,
    tri_gate,
    tri_out,
    pair_proj,
    atom_act,
    atom_cond,
    cond_pair,
    pair_mlp,
    bias_proj,
    block_weights,
    atom_token,
    atom_mask,
    key_start,
    key_tiles,
):
    tok_dev, tokens, _ = pair.shape
    groups = lax.axis_size("tok")
    ch = tri_in.shape[2]
    shard = lax.axis_index("tok")
    core = lax.axis_index("atm")
    up = [(i, i + 1) for i in range(groups - 1)]
    down = [(i + 1, i) for i in range(groups - 1)]

    half = tokens // 2
    chunk = 8 * tok_dev
    swap = [(0, 1), (1, 0)]
    own = lax.dynamic_slice_in_dim(pair, core * half, half, 1)
    low = lax.ppermute(own, "tok", up)
    w = jnp.swapaxes(tri_in, 1, 2).reshape(4 * ch, -1)
    own_left, own_right = project(own, w, chunk)
    own_prod = product(own_left, own_right, ch)
    own_other = lax.ppermute(own_prod, "atm", swap)

    padded = jnp.pad(pair, ((0, 0), (tok_dev, tok_dev), (0, 0)))
    band = lax.dynamic_slice_in_dim(padded, shard * tok_dev, 3 * tok_dev, 1)
    band = band.reshape(tok_dev, 3, tok_dev, -1)
    band = jnp.concatenate([band[:, 1:2], band[:, 0:1], band[:, 2:3]], axis=1)
    band = jnp.pad(band, ((0, 0), (0, 0), (0, SLOT - tok_dev), (0, 0)))
    band = band.reshape(tok_dev, 3 * SLOT, -1)
    gate = gates_of(band, tri_gate)

    atoms = atom_act.shape[0]
    heads = bias_proj.shape[2]
    device = shard * lax.axis_size("atm") + core
    labels = jnp.stack([atom_token, atom_mask], 1).astype(jnp.float32)
    relu_cond = jax.nn.relu(atom_cond)
    query_term = jnp.dot(relu_cond, cond_pair[0], preferred_element_type=jnp.float32)
    key_term = jnp.dot(relu_cond, cond_pair[1], preferred_element_type=jnp.float32)
    keys = jnp.concatenate([key_term, labels], 1)
    keys = with_halo(keys, ((("tok", "atm"), 0),), HALO).T
    offsets = key_start - device * atoms + HALO
    projections = jnp.swapaxes(bias_proj, 0, 1).reshape(bias_proj.shape[1], -1).astype(jnp.float32)
    mixed = jnp.dot(
        pair_mlp.astype(jnp.float32), projections, precision=lax.Precision.HIGHEST
    )
    starts = jnp.repeat(offsets, QUERY_ATOMS).astype(jnp.float32)
    queries = jnp.concatenate([query_term, labels[:, :1], starts[:, None]], 1)
    mix = jnp.concatenate([projections, mixed], 0)
    early = (mix, queries, keys, band, gate, own_prod, own_other, pair_proj.T)
    low, early = lax.optimization_barrier((low, early))
    mix, queries, keys, band, gate, own_prod, own_other, proj_t = early

    low_left, low_right = project(low, w, chunk)
    back = product(low_left, own_right, ch)
    back = (back + lax.ppermute(back, "atm", swap)).astype(jnp.bfloat16)
    own_left, back = lax.optimization_barrier((own_left, back))
    back = lax.ppermute(back, "tok", down)
    main = product(own_left, low_right, ch)
    other = lax.ppermute(main, "atm", swap)
    back = back.astype(jnp.float32)
    pair_band, table = tail(own_prod, own_other, main, other, back, band, gate, tri_out, proj_t)
    atoms_out = atoms_part(
        mix,
        table,
        queries,
        keys,
        atom_act,
        atom_cond,
        block_weights,
        groups * lax.axis_size("atm"),
        heads,
        tok_dev,
    )
    return (pair_band, atoms_out)


def solution(mesh):
    in_specs = (
        P("tok", None, None),
        P(),
        P(),
        P(),
        P(),
        P(("tok", "atm"), None),
        P(("tok", "atm"), None),
        P(),
        P(),
        P(),
        P(),
        P(("tok", "atm")),
        P(("tok", "atm")),
        P(("tok", "atm")),
        P(("tok", "atm"), None),
    )
    out_specs = (P("tok", None, None), P(("tok", "atm"), None))
    return jax.shard_map(local, mesh=mesh, in_specs=in_specs, out_specs=out_specs, check_vma=False)
```
